256 devices in a mesh: row: 16 (over z, core), col: 16 (over y, x).
Axes of the slice: x: 4, y: 4, z: 8, core: 2. Of those that a mesh axis runs over, the one named last changes fastest.
Arguments:
- eigvecs: bfloat16 [98304, 8192], P('row', 'col'), may hold values from -6 to 6
- panels: bfloat16 [2, 128, 98304], P(None, 'col', 'row'), may hold values from -0.078125 to 0.078125
- tfactors: float32 [2, 128, 128], replicated, may hold values from -0.1 to 0.5, as said below
- offsets: int32 [2], replicated, may hold values from 0 to 98176
Outputs:
- result: bfloat16 [98304, 8192], P('row', 'col')
The draws below stay inside these ranges and needn't reach their ends.
Inputs may be any that keep to these rules, and one draw needn't show every extreme that they name: Entries below the diagonal of each tfactors[p] are zero.
All inputs are finite; a program needn't handle non-finite values.
Results may differ from the reference program's by a relative error of at most 0.0034.
Values may be sent and summed in bfloat16 or wider, within the bound.
A program may use at most 64 MiB of HBM per device.

```python
import jax
import jax.numpy as jnp
from jax import lax

NB = 128
PANELS = 2
RD = 6144
KD = 512
N = 98304
K = 8192
N_ROW = 16
N_COL = 16


def draw_tfactors(key, part):
    key = jax.random.fold_in(key, 7)
    key_off, key_diag = jax.random.split(key)
    shape = (PANELS, NB, NB)
    above = 0.02 * jnp.clip(jax.random.normal(key_off, shape, jnp.float32), -5.0, 5.0)
    diag = 0.3 + 0.2 * jax.random.uniform(key_diag, (PANELS, NB, 1), jnp.float32)
    row_index = lax.broadcasted_iota(jnp.int32, shape, 1)
    col_index = lax.broadcasted_iota(jnp.int32, shape, 2)
    strict = jnp.where(col_index > row_index, above, 0.0)
    ondiag = jnp.where(col_index == row_index, diag, 0.0)
    return (strict + ondiag).astype(jnp.float32)


def block_scale(rng, shape, cuts, smallest, high):
    loudness = 1.0
    for dim, parts in cuts:
        steps = jax.random.uniform(jax.random.fold_in(jax.random.fold_in(rng, 6), dim), (parts,), jnp.float32, smallest / len(cuts), high / len(cuts))
        loudness = loudness * jnp.repeat(jnp.exp(steps), shape[dim] // parts).reshape((-1,) + (1,) * (len(shape) - 1 - dim))
    return loudness


def bell_draw(key, shape, scale, most, pieces=(), kind=jnp.bfloat16):
    factor_of = block_scale(key, shape, pieces, -0.22, 0.18) if pieces else 1.0
    values = jax.random.normal(key, shape, jnp.float32) * scale * factor_of
    return jnp.minimum(jnp.maximum(values, -most), most).astype(kind)


def setup_inputs(seed: int = 0) -> dict:
    key_of = jax.random.split(jax.random.key(seed), 5)
    return {
        "eigvecs": bell_draw(key_of[0], (N, K), 1.0, 6.0, ((0, 16), (1, 16))),
        "panels": bell_draw(key_of[1], (PANELS, NB, N), (RD * N_ROW // 16) ** -0.5, 0.078125, ((1, 16), (2, 16))),
        "tfactors": draw_tfactors(jax.random.fold_in(key_of[4], 71), 0),
        "offsets": jax.random.randint(key_of[3], (PANELS,), 0, RD * N_ROW - NB + 1).astype(jnp.int32),
    }


def reflectors(panels, offsets):
    position = lax.broadcasted_iota(jnp.int32, (NB, N), 1)
    column = lax.broadcasted_iota(jnp.int32, (NB, N), 0)
    built = []
    for p in range(PANELS):
        pivot = offsets[p] + column
        unit = jnp.where(position == pivot, 1.0, 0.0).astype(jnp.bfloat16)
        built.append(jnp.where(position > pivot, panels[p], unit))
    return built


def reference(eigvecs, panels, tfactors, offsets):
    first, second = reflectors(panels, offsets)
    upper = jnp.triu(tfactors)
    high = lax.Precision.HIGHEST
    cross = lax.dot_general(first, second, (((1,), (1,)), ((), ())), preferred_element_type=jnp.float32)
    stacked = jnp.concatenate([second, first], axis=0)
    dims = (((0,), (0,)), ((), ()))

    def one_block(b, output):
        start = (b * KD).astype(jnp.int32)
        block = lax.dynamic_slice_in_dim(eigvecs, start, KD, 1)
        coeff_one = jnp.dot(second, block, preferred_element_type=jnp.float32)
        shift_one = jnp.dot(upper[1], coeff_one, precision=high).astype(jnp.bfloat16)
        coeff_zero = jnp.dot(first, block, preferred_element_type=jnp.float32) - jnp.dot(cross, shift_one.astype(jnp.float32), precision=high)
        shift_zero = jnp.dot(upper[0], coeff_zero, precision=high).astype(jnp.bfloat16)
        shifts = jnp.concatenate([shift_one, shift_zero], axis=0)
        final = block.astype(jnp.float32) - lax.dot_general(stacked, shifts, dims, preferred_element_type=jnp.float32)
        return lax.dynamic_update_slice_in_dim(output, final.astype(jnp.bfloat16), start, 1)

    output = jnp.zeros((N, K), jnp.bfloat16)
    return lax.fori_loop(jnp.int32(0), jnp.int32(N_COL), one_block, output)
```

```python
import jax
import jax.numpy as jnp
from jax import lax
from jax.experimental import pallas as pl
from jax.experimental.pallas import tpu as pltpu
from jax.sharding import PartitionSpec as P

MESH = pl.DeviceIdType.MESH
F32 = jnp.float32
BF16 = jnp.bfloat16
HIGH = lax.Precision.HIGHEST

NB = 128
RD = 6144
KD = 512
NX = 4
NZ = 8
OWN = 16
Q = 2 * NB
HALF = RD // 2
QUART = RD // 4
CHUNK = NX * OWN
KT = 1536
ORDER = (0, 1, 3, 2)


def expand(a, panel):
    zero = jnp.zeros((8, a.shape[1]), a.dtype)
    rows = []
    for sx in range(NX):
        for sy in range(NX):
            o = (sy * NX + sx) * 8
            pair = [zero, zero]
            pair[panel] = a[o : o + 8, :]
            rows += pair
    return jnp.concatenate(rows, axis=0)


def gather_and_reduce(
    offsets, panels, eig, tf, H, YT, E,
    pbuf, tfbuf, T, gt, ws, cbuf, xs, zbuf, cg, crow, Cq,
    local_sem, a_send, a_recv, b_send, b_recv,
    w_send, w_recv, z_send, z_recv, g_send, g_recv, c_send, c_recv, y_send, y_recv, s_send, s_recv,
):
    col = lax.axis_index("col")
    row = lax.axis_index("row")
    x, y = col % NX, col // NX
    z, core = row // 2, row % 2

    def at_x(d):
        return {"col": y * NX + (x + d) % NX}

    def at_y(d):
        return {"col": ((y + d) % NX) * NX + x}

    def at_z(d):
        return {"row": ((z + d) % NZ) * 2 + core}

    sibling = {"row": z * 2 + (1 - core)}

    load_panels = pltpu.make_async_copy(panels, pbuf, local_sem.at[0])
    load_tf = pltpu.make_async_copy(tf, tfbuf, local_sem.at[1])
    load_eig = pltpu.make_async_copy(eig, E, local_sem.at[2])
    load_panels.start()
    load_tf.start()
    load_eig.start()

    Cq[...] = jnp.zeros((Q, Q), F32)
    barrier = pltpu.get_barrier_semaphore()
    for d in range(1, 16):
        pl.semaphore_signal(barrier, inc=1, device_id={"col": (col + d) % 16}, device_id_type=MESH)
        pl.semaphore_signal(barrier, inc=1, device_id={"row": (row + d) % 16}, device_id_type=MESH)

    slot = pl.multiple_of((x * NX + y) * OWN, OWN)
    load_panels.wait()
    step = 512
    for c0 in range(0, RD, step):
        position = row * RD + c0 + lax.broadcasted_iota(jnp.int32, (8, step), 1)
        parts = []
        for p in range(2):
            pivot = offsets[p] + col * 8 + lax.broadcasted_iota(jnp.int32, (8, step), 0)
            v = pbuf[p, :, c0 : c0 + step].astype(F32)
            parts.append(jnp.where(position > pivot, v, jnp.where(position == pivot, 1.0, 0.0)))
        H[pl.ds(slot, OWN), c0 : c0 + step] = jnp.concatenate(parts, axis=0).astype(BF16)

    pl.semaphore_wait(barrier, 30)

    def part(dx, dy, lo, n):
        s = ((x + dx) % NX) * NX + (y + dy) % NX
        return H.at[pl.ds(pl.multiple_of(s * OWN, OWN), OWN), lo : lo + n]

    sent = []

    def send(ref, sems, i, dev):
        send_sem, recv_sem = sems
        cp = pltpu.make_async_remote_copy(ref, ref, send_sem.at[i], recv_sem.at[i], device_id=dev, device_id_type=MESH)
        cp.start()
        sent.append(cp)

    def recv(ref, sems, i):
        send_sem, recv_sem = sems
        pltpu.make_async_remote_copy(ref, ref, send_sem.at[i], recv_sem.at[i], device_id=sibling, device_id_type=MESH).wait_recv()

    class Half:
        def __init__(self, lo, sems, first, second, turn):
            self.lo, self.sems, self.first, self.second, self.turn = lo, sems, first, second, turn

        def ref(self, d1, d2, piece=None):
            lo, n = (self.lo, HALF) if piece is None else (self.lo + piece * QUART, QUART)
            return part(d1, d2, lo, n) if not self.turn else part(d2, d1, lo, n)

        def send_own(self):
            send(self.ref(0, 0), self.sems, 0, self.first(1))
            send(self.ref(0, 0), self.sems, 1, self.first(-1))

        def recv_own(self):
            recv(self.ref(-1, 0), self.sems, 0)
            recv(self.ref(1, 0), self.sems, 1)

        def send_far(self):
            send(self.ref(-1, 0, 0), self.sems, 2, self.first(1))
            send(self.ref(1, 0, 1), self.sems, 3, self.first(-1))

        def recv_far(self):
            recv(self.ref(2, 0, 0), self.sems, 2)
            recv(self.ref(2, 0, 1), self.sems, 3)

        def send_line(self, d):
            send(self.ref(d, 0), self.sems, 4 + 2 * d, self.second(1))
            send(self.ref(d, 0), self.sems, 5 + 2 * d, self.second(-1))

        def recv_line(self, d):
            recv(self.ref(d, -1), self.sems, 4 + 2 * d)
            recv(self.ref(d, 1), self.sems, 5 + 2 * d)

        def send_far_line(self, d):
            send(self.ref(d, -1, 0), self.sems, 12 + 2 * d, self.second(1))
            send(self.ref(d, 1, 1), self.sems, 13 + 2 * d, self.second(-1))

        def recv_far_line(self, d):
            recv(self.ref(d, 2, 0), self.sems, 12 + 2 * d)
            recv(self.ref(d, 2, 1), self.sems, 13 + 2 * d)

    a = Half(0, (a_send, a_recv), at_x, at_y, False)
    b = Half(HALF, (b_send, b_recv), at_y, at_x, True)

    def products(k):
        dx = ORDER[k]
        r0 = pl.multiple_of(((x + dx) % NX) * CHUNK, CHUNK)
        ws[k] = jnp.zeros((CHUNK, KD), F32)
        gt[pl.ds(r0, CHUNK), :] = jnp.zeros((CHUNK, OWN), F32)

        def body(t, _):
            k0 = pl.multiple_of(t * KT, KT)
            h = H[pl.ds(r0, CHUNK), pl.ds(k0, KT)]
            ws[k] += jnp.dot(h, E[pl.ds(k0, KT), :], preferred_element_type=F32)
            own = H[pl.ds(slot, OWN), pl.ds(k0, KT)]
            gt[pl.ds(r0, CHUNK), :] += lax.dot_general(h, own, (((1,), (1,)), ((), ())), preferred_element_type=F32)
            return 0

        lax.fori_loop(0, RD // KT, body, 0)
        theirs = pl.ds(pl.multiple_of((1 - core) * (KD // 2), KD // 2), KD // 2)
        cp = pltpu.make_async_remote_copy(
            ws.at[k, :, theirs], cbuf.at[k], w_send.at[k], w_recv.at[k], device_id=sibling, device_id_type=MESH
        )
        cp.start()
        sent.append(cp)

    def scatter(k):
        pltpu.make_async_remote_copy(
            cbuf.at[k], cbuf.at[k], w_send.at[k], w_recv.at[k], device_id=sibling, device_id_type=MESH
        ).wait_recv()
        mine = pl.ds(pl.multiple_of(core * (KD // 2), KD // 2), KD // 2)
        s = ws[k, :, mine] + cbuf[k]
        xs[k] = jnp.concatenate([s[:, :128], s[:, 128:]], axis=0).T
        for d in range(1, NZ):
            r = pl.multiple_of(((z + d) % NZ) * 16, 16)
            cp = pltpu.make_async_remote_copy(
                xs.at[k, pl.ds(r, 16)], zbuf.at[k, d], z_send.at[k, d], z_recv.at[k, d],
                device_id=at_z(d), device_id_type=MESH,
            )
            cp.start()
            sent.append(cp)

    def collect(k):
        total = xs[k, pl.ds(pl.multiple_of(z * 16, 16), 16)]
        for d in range(1, NZ):
            ref = zbuf.at[k, d]
            pltpu.make_async_remote_copy(
                ref, ref, z_send.at[k, d], z_recv.at[k, d], device_id=sibling, device_id_type=MESH
            ).wait_recv()
            total = total + zbuf[k, d]
        return total

    a.send_own()
    b.send_own()
    a.send_line(0)
    b.send_line(0)
    load_tf.wait()
    for p in range(2):
        tri = lax.broadcasted_iota(jnp.int32, (NB, NB), 0) <= lax.broadcasted_iota(jnp.int32, (NB, NB), 1)
        u = jnp.where(tri, tfbuf[p], 0.0)
        T[p] = expand(expand(u, p).T, p)
    a.recv_own()
    a.send_far()
    a.send_line(1)
    a.send_line(3)
    b.recv_own()
    b.send_far()
    b.send_line(1)
    b.send_line(3)
    a.recv_line(0)
    a.send_far_line(0)
    b.recv_far()
    b.send_line(2)
    b.recv_line(0)
    b.send_far_line(0)
    load_eig.wait()
    a.recv_far_line(0)
    products(0)
    a.recv_line(1)
    a.send_far_line(1)
    a.recv_line(3)
    a.send_far_line(3)
    a.recv_far()
    a.send_line(2)
    b.recv_line(1)
    b.send_far_line(1)
    b.recv_line(3)
    b.send_far_line(3)
    scatter(0)
    b.recv_line(2)
    b.send_far_line(2)
    a.recv_far_line(1)
    products(1)
    a.recv_line(2)
    a.send_far_line(2)
    a.recv_far_line(3)
    products(2)
    scatter(1)
    scatter(2)
    a.recv_far_line(2)
    for d in range(NX):
        b.recv_far_line(d)
    products(3)

    cg[...] = gt[...].T[:8, :]
    for d in range(1, 16):
        cp = pltpu.make_async_remote_copy(
            cg, crow.at[d], g_send.at[d], g_recv.at[d], device_id={"row": (row + d) % 16}, device_id_type=MESH
        )
        cp.start()
        sent.append(cp)
    scatter(3)
    total = cg[...]
    for d in range(1, 16):
        ref = crow.at[d]
        pltpu.make_async_remote_copy(
            ref, ref, g_send.at[d], g_recv.at[d], device_id=sibling, device_id_type=MESH
        ).wait_recv()
        total = total + crow[d]
    Cq[pl.ds(slot, 8), :] = total

    def cross_rows(d):
        o = (col + 16 - d) % 16
        return Cq.at[pl.ds(pl.multiple_of(((o % NX) * NX + o // NX) * OWN, OWN), 8), :]

    for d in range(1, 16):
        cp = pltpu.make_async_remote_copy(
            cross_rows(0), cross_rows(0), c_send.at[d], c_recv.at[d],
            device_id={"col": (col + d) % 16}, device_id_type=MESH,
        )
        cp.start()
        sent.append(cp)

    by_chunk = {ORDER[k]: collect(k) for k in range(NX)}
    wt = jnp.concatenate(
        [jnp.concatenate([by_chunk[d][:, h * 64 : h * 64 + 64] for d in range(NX)], axis=1) for h in range(2)], axis=0
    )
    wt = pltpu.roll(wt, x * CHUNK, 1)
    y1 = jnp.dot(wt, T[1], precision=HIGH, preferred_element_type=F32).astype(BF16).astype(F32)
    for d in range(1, 16):
        ref = cross_rows(d)
        pltpu.make_async_remote_copy(
            ref, ref, c_send.at[d], c_recv.at[d], device_id=sibling, device_id_type=MESH
        ).wait_recv()
    w0 = wt - lax.dot_general(y1, Cq[...], (((1,), (1,)), ((), ())), precision=HIGH, preferred_element_type=F32)
    y0 = jnp.dot(w0, T[0], precision=HIGH, preferred_element_type=F32)
    yt = (y1 + y0).astype(BF16)

    def shift_rows(dz, h):
        return YT.at[pl.ds(pl.multiple_of(core * 256 + h * 128 + ((z + dz) % NZ) * 16, 16), 16), :]

    for h in range(2):
        YT[pl.ds(pl.multiple_of(core * 256 + h * 128 + z * 16, 16), 16), :] = yt[h * 16 : h * 16 + 16]
        for d in range(1, NZ):
            ref = shift_rows(0, h)
            cp = pltpu.make_async_remote_copy(
                ref, ref, y_send.at[h, d], y_recv.at[h, d], device_id=at_z(d), device_id_type=MESH
            )
            cp.start()
            sent.append(cp)
    for h in range(2):
        for d in range(1, NZ):
            ref = shift_rows(-d, h)
            pltpu.make_async_remote_copy(
                ref, ref, y_send.at[h, d], y_recv.at[h, d], device_id=sibling, device_id_type=MESH
            ).wait_recv()
    ours = YT.at[pl.ds(pl.multiple_of(core * 256, 256), 256), :]
    theirs = YT.at[pl.ds(pl.multiple_of((1 - core) * 256, 256), 256), :]
    cp = pltpu.make_async_remote_copy(ours, ours, s_send, s_recv, device_id=sibling, device_id_type=MESH)
    cp.start()
    sent.append(cp)
    pltpu.make_async_remote_copy(theirs, theirs, s_send, s_recv, device_id=sibling, device_id_type=MESH).wait_recv()
    for cp in sent:
        cp.wait_send()


ROWS = 1024


def apply_shift(H, YT, E, out, shift):
    i = pl.program_id(0)

    @pl.when(i == 0)
    def _():
        shift[...] = YT[...].T

    rows = pl.ds(pl.multiple_of(i * ROWS, ROWS), ROWS)
    term = lax.dot_general(H[:, rows], shift[...], (((0,), (0,)), ((), ())), preferred_element_type=F32)
    out[...] = (E[rows, :].astype(F32) - term).astype(BF16)


def local(eigvecs, panels, tfactors, offsets):
    anywhere = pl.BlockSpec(memory_space=pl.ANY)
    dma = pltpu.SemaphoreType.DMA
    H, YT, E = pl.pallas_call(
        gather_and_reduce,
        out_shape=[
            pltpu.VMEM((Q, RD), BF16),
            pltpu.VMEM((KD, Q), BF16),
            pltpu.VMEM((RD, KD), BF16),
        ],
        in_specs=[pl.BlockSpec(memory_space=pltpu.SMEM), anywhere, anywhere, anywhere],
        out_specs=[pl.BlockSpec(memory_space=pltpu.VMEM)] * 3,
        scratch_shapes=[
            pltpu.VMEM((2, 8, RD), BF16),
            pltpu.VMEM((2, NB, NB), F32),
            pltpu.VMEM((2, Q, Q), F32),
            pltpu.VMEM((Q, OWN), F32),
            pltpu.VMEM((NX, CHUNK, KD), F32),
            pltpu.VMEM((NX, CHUNK, KD // 2), F32),
            pltpu.VMEM((NX, 128, 128), F32),
            pltpu.VMEM((NX, NZ, 16, 128), F32),
            pltpu.VMEM((8, Q), F32),
            pltpu.VMEM((16, 8, Q), F32),
            pltpu.VMEM((Q, Q), F32),
            dma((3,)),
            dma((20,)), dma((20,)), dma((20,)), dma((20,)),
            dma((NX,)), dma((NX,)),
            dma((NX, NZ)), dma((NX, NZ)),
            dma((16,)), dma((16,)), dma((16,)), dma((16,)),
            dma((2, NZ)), dma((2, NZ)),
            dma, dma,
        ],
        compiler_params=pltpu.CompilerParams(
            collective_id=0, has_side_effects=True, vmem_limit_bytes=40 * 1024 * 1024
        ),
        name="gather_and_reduce",
    )(offsets, panels, eigvecs, tfactors)
    whole = pl.BlockSpec(memory_space=pltpu.VMEM)
    return pl.pallas_call(
        apply_shift,
        grid=(RD // ROWS,),
        out_shape=jax.ShapeDtypeStruct((RD, KD), BF16),
        in_specs=[whole, whole, whole],
        out_specs=pl.BlockSpec((ROWS, KD), lambda i: (i, 0)),
        scratch_shapes=[pltpu.VMEM((Q, KD), BF16)],
        compiler_params=pltpu.CompilerParams(vmem_limit_bytes=40 * 1024 * 1024),
        name="apply_shift",
    )(H, YT, E)


def solution(mesh):
    return jax.shard_map(
        local,
        mesh=mesh,
        in_specs=(P("row", "col"), P(None, "col", "row"), P(), P()),
        out_specs=P("row", "col"),
        check_vma=False,
    )
```

```python
import jax
import jax.numpy as jnp
from jax import lax
from jax.experimental import pallas as pl
from jax.experimental.pallas import tpu as pltpu
from jax.sharding import PartitionSpec as P

MESH = pl.DeviceIdType.MESH
F32 = jnp.float32
BF16 = jnp.bfloat16
HIGH = lax.Precision.HIGHEST

NB = 128
RD = 6144
KD = 512
KH = KD // 2
NX = 4
NZ = 8
OWN = 8
SLOTS = NX * NX
HALF = RD // 2
QUART = RD // 4
CHUNK = NX * OWN
KT = 1536
ORDER = (0, 1, 3, 2)


def dot(a, b, dims=((1,), (0,)), precision=None):
    return lax.dot_general(a, b, (dims, ((), ())), precision=precision, preferred_element_type=F32)


def by_place(a):
    return jnp.concatenate([a[(sy * NX + sx) * OWN :][:OWN, :] for sx in range(NX) for sy in range(NX)], axis=0)


def gather_and_reduce(
    offsets, panels, eig, tf, HT, Y, E,
    H, obuf, pbuf, tfbuf, T, ct, w1, c1, x1, z1, w0, c0, x0, z0, crow, C, ybuf,
    local_sem, a_send, a_recv, b_send, b_recv,
    w_send, w_recv, z_send, z_recv, g_send, g_recv, c_send, c_recv, y_send, y_recv, f_send, f_recv,
):
    col = lax.axis_index("col")
    row = lax.axis_index("row")
    x, y = col % NX, col // NX
    z, core = row // 2, row % 2

    def at_x(d):
        return {"col": y * NX + (x + d) % NX}

    def at_y(d):
        return {"col": ((y + d) % NX) * NX + x}

    def at_z(d):
        return {"row": ((z + d) % NZ) * 2 + core}

    sibling = {"row": z * 2 + (1 - core)}

    load_panels = pltpu.make_async_copy(panels, pbuf, local_sem.at[0])
    load_offsets = pltpu.make_async_copy(offsets, obuf, local_sem.at[3])
    load_tf = pltpu.make_async_copy(tf, tfbuf, local_sem.at[1])
    load_eig = pltpu.make_async_copy(eig, E, local_sem.at[2])
    load_panels.start()
    load_offsets.start()
    load_tf.start()
    load_eig.start()

    barrier = pltpu.get_barrier_semaphore()
    for d in range(1, 16):
        pl.semaphore_signal(barrier, inc=1, device_id={"col": (col + d) % 16}, device_id_type=MESH)
        pl.semaphore_signal(barrier, inc=1, device_id={"row": (row + d) % 16}, device_id_type=MESH)

    slot = x * NX + y
    load_panels.wait()
    load_offsets.wait()
    step = 512
    for p in range(2):
        pivot = obuf[p] + col * OWN + lax.broadcasted_iota(jnp.int32, (OWN, step), 0)
        for s in range(0, RD, step):
            position = row * RD + s + lax.broadcasted_iota(jnp.int32, (OWN, step), 1)
            v = pbuf[p, :, s : s + step].astype(F32)
            v = jnp.where(position > pivot, v, jnp.where(position == pivot, 1.0, 0.0))
            H[p, slot, :, s : s + step] = v.astype(BF16)

    pl.semaphore_wait(barrier, 30)

    def part(p, dx, dy, lo, n):
        return H.at[p, ((x + dx) % NX) * NX + (y + dy) % NX, :, lo : lo + n]

    sent = []

    def send(src, dst, send_sem, recv_sem, dev):
        cp = pltpu.make_async_remote_copy(src, dst, send_sem, recv_sem, device_id=dev, device_id_type=MESH)
        cp.start()
        sent.append(cp)

    def recv(ref, send_sem, recv_sem):
        pltpu.make_async_remote_copy(
            ref, ref, send_sem, recv_sem, device_id=sibling, device_id_type=MESH
        ).wait_recv()

    class Half:
        def __init__(self, p, lo, sems, first, second, turn):
            self.p, self.lo, self.sems = p, lo, sems
            self.first, self.second, self.turn = first, second, turn

        def ref(self, d1, d2, piece=None):
            lo, n = (self.lo, HALF) if piece is None else (self.lo + piece * QUART, QUART)
            return part(self.p, d2, d1, lo, n) if self.turn else part(self.p, d1, d2, lo, n)

        def put(self, ref, i, dev):
            send(ref, ref, self.sems[0].at[self.p, i], self.sems[1].at[self.p, i], dev)

        def get(self, ref, i):
            recv(ref, self.sems[0].at[self.p, i], self.sems[1].at[self.p, i])

        def send_own(self):
            self.put(self.ref(0, 0), 0, self.first(1))
            self.put(self.ref(0, 0), 1, self.first(-1))

        def recv_own(self):
            self.get(self.ref(-1, 0), 0)
            self.get(self.ref(1, 0), 1)

        def send_far(self):
            self.put(self.ref(-1, 0, 0), 2, self.first(1))
            self.put(self.ref(1, 0, 1), 3, self.first(-1))

        def recv_far(self):
            self.get(self.ref(2, 0, 0), 2)
            self.get(self.ref(2, 0, 1), 3)

        def send_line(self, d):
            self.put(self.ref(d, 0), 4 + 2 * d, self.second(1))
            self.put(self.ref(d, 0), 5 + 2 * d, self.second(-1))

        def recv_line(self, d):
            self.get(self.ref(d, -1), 4 + 2 * d)
            self.get(self.ref(d, 1), 5 + 2 * d)

        def send_far_line(self, d):
            self.put(self.ref(d, -1, 0), 12 + 2 * d, self.second(1))
            self.put(self.ref(d, 1, 1), 13 + 2 * d, self.second(-1))

        def recv_far_line(self, d):
            self.get(self.ref(d, 2, 0), 12 + 2 * d)
            self.get(self.ref(d, 2, 1), 13 + 2 * d)

        def own_on(self):
            self.recv_own()
            self.send_far()
            self.send_line(1)
            self.send_line(3)

        def line_on(self, *ds):
            for d in ds:
                self.recv_line(d)
                self.send_far_line(d)

        def far_on(self):
            self.recv_far()
            self.send_line(2)

    halves = {
        p: (
            Half(p, 0, (a_send, a_recv), at_x, at_y, False),
            Half(p, HALF, (b_send, b_recv), at_y, at_x, True),
        )
        for p in range(2)
    }
    a0, b0 = halves[0]
    a1, b1 = halves[1]

    theirs = pl.ds(pl.multiple_of((1 - core) * KH, KH), KH)
    mine = pl.ds(pl.multiple_of(core * KH, KH), KH)

    def products_one():
        for t in range(RD // KT):
            k = slice(t * KT, (t + 1) * KT)
            h = H[1, :, :, k].reshape(NB, KT)
            s = dot(h, E[k, :])
            c = dot(h, H[0, slot, :, k], ((1,), (1,)))
            if t:
                s, c = s + w1[...], c + ct[...]
            w1[...] = s
            ct[...] = c
        crow[0] = ct[...].T
        for d in range(1, 16):
            send(crow.at[0], crow.at[d], g_send.at[d], g_recv.at[d], {"row": (row + d) % 16})
        send(w1.at[:, theirs], c1, w_send.at[NX], w_recv.at[NX], sibling)

    def scatter_one():
        recv(c1, w_send.at[NX], w_recv.at[NX])
        x1[...] = (w1[:, mine] + c1[...]).T.reshape(4, 64, NB)
        for d in (4, 3, 5, 2, 6, 1, 7):
            r = pl.multiple_of(((z + d) % NZ) * 8, 8)
            send(x1.at[:, pl.ds(r, 8), :], z1.at[d], z_send.at[NX, d], z_recv.at[NX, d], at_z(d))

    def collect_one():
        total = x1[:, pl.ds(pl.multiple_of(z * 8, 8), 8), :]
        for d in range(1, NZ):
            recv(z1.at[d], z_send.at[NX, d], z_recv.at[NX, d])
            total = total + z1[d]
        return total.reshape(32, NB)

    def products(k, lo, hi):
        sx = (x + ORDER[k]) % NX
        for t in range(lo // KT, hi // KT):
            ks = slice(t * KT, (t + 1) * KT)
            s = dot(H[0, pl.ds(sx * NX, NX), :, ks].reshape(CHUNK, KT), E[ks, :])
            w0[k] = s + w0[k] if t else s

    def swap(k):
        send(w0.at[k, :, theirs], c0.at[k], w_send.at[k], w_recv.at[k], sibling)

    def scatter(k):
        recv(c0.at[k], w_send.at[k], w_recv.at[k])
        s = w0[k, :, mine] + c0[k]
        x0[k] = jnp.concatenate([s[:, g * 64 : g * 64 + 64] for g in range(4)], axis=0).T
        for d in (4, 3, 5, 2, 6, 1, 7):
            r = pl.multiple_of(((z + d) % NZ) * 8, 8)
            send(x0.at[k, pl.ds(r, 8), :], z0.at[k, d], z_send.at[k, d], z_recv.at[k, d], at_z(d))

    def collect(k):
        total = x0[k, pl.ds(pl.multiple_of(z * 8, 8), 8), :]
        for d in range(1, NZ):
            recv(z0.at[k, d], z_send.at[k, d], z_recv.at[k, d])
            total = total + z0[k, d]
        return jnp.concatenate([total[:, g * CHUNK : (g + 1) * CHUNK] for g in range(4)], axis=0)

    def cross_sum():
        total = crow[0]
        for d in range(1, 16):
            recv(crow.at[d], g_send.at[d], g_recv.at[d])
            total = total + crow[d]
        C[slot] = total
        for d in range(1, 16):
            send(C.at[slot], C.at[slot], c_send.at[d], c_recv.at[d], {"col": (col + d) % 16})

    def cross_recv():
        for d in range(1, 16):
            o = (col + 16 - d) % 16
            recv(C.at[(o % NX) * NX + o // NX], c_send.at[d], c_recv.at[d])
        return C[...].reshape(NB, NB)

    def spread(p, value):
        ref = ybuf.at[p, core * NZ + z]
        ybuf[p, core * NZ + z] = value
        for d in (4, 3, 5, 2, 6, 1, 7):
            send(ref, ref, y_send.at[p, d], y_recv.at[p, d], at_z(d))
        send(ref, ref, f_send.at[p, 0], f_recv.at[p, 0], sibling)

    def pass_on(p):
        for d in (1, 7, 2, 6, 3, 5, 4):
            ref = ybuf.at[p, core * NZ + (z + NZ - d) % NZ]
            recv(ref, y_send.at[p, d], y_recv.at[p, d])
            send(ref, ref, f_send.at[p, d], f_recv.at[p, d], sibling)

    def place(p, c):
        v = [ybuf[p, c * NZ + i].astype(F32) for i in range(NZ)]
        v = jnp.concatenate([v[i][g * 8 : g * 8 + 8, :] for g in range(4) for i in range(NZ)], axis=0)
        Y[p * NB : (p + 1) * NB, pl.ds(pl.multiple_of(c * KH, KH), KH)] = v.T.astype(BF16)

    def finish(p):
        place(p, core)
        for d in range(NZ):
            recv(ybuf.at[p, (1 - core) * NZ + (z + NZ - d) % NZ], f_send.at[p, d], f_recv.at[p, d])
        place(p, 1 - core)

    def turn(p):
        for r in range(0, RD, 512):
            HT[r : r + 512, p * NB : (p + 1) * NB] = H[p, :, :, r : r + 512].reshape(NB, 512).T

    a1.send_own()
    b1.send_own()
    a1.send_line(0)
    b1.send_line(0)
    load_tf.wait()
    for p in range(2):
        tri = lax.broadcasted_iota(jnp.int32, (NB, NB), 0) <= lax.broadcasted_iota(jnp.int32, (NB, NB), 1)
        T[p] = by_place(by_place(jnp.where(tri, tfbuf[p], 0.0)).T)
    a0.send_own()
    b0.send_own()
    a0.send_line(0)
    b0.send_line(0)
    a1.own_on()
    b1.own_on()
    a1.line_on(0)
    b1.line_on(0)
    a1.far_on()
    b1.far_on()
    a0.own_on()
    b0.own_on()
    a1.line_on(1, 3)
    b1.line_on(1, 3)
    a0.line_on(0)
    b0.line_on(0)
    a1.line_on(2)
    b1.line_on(2)
    a0.far_on()
    b0.far_on()
    a0.line_on(1, 3)
    b0.line_on(1, 3)
    load_eig.wait()
    for d in range(NX):
        a1.recv_far_line(d)
        b1.recv_far_line(d)
    products_one()
    a0.line_on(2)
    b0.line_on(2)
    scatter_one()
    a0.recv_far_line(0)
    products(0, 0, RD)
    swap(0)
    a0.recv_far_line(1)
    products(1, 0, RD)
    swap(1)
    cross_sum()
    a0.recv_far_line(3)
    products(2, 0, RD)
    swap(2)
    scatter(0)
    scatter(1)
    a0.recv_far_line(2)
    products(3, 0, HALF)
    for d in range(NX):
        b0.recv_far_line(d)
    products(3, HALF, RD)
    swap(3)
    scatter(2)
    y1 = dot(collect_one(), T[1], precision=HIGH).astype(BF16)
    spread(1, y1)
    scatter(3)
    turn(1)
    turn(0)
    cross = cross_recv()
    shift = dot(y1.astype(F32), cross, ((1,), (1,)), precision=HIGH)
    parts = {ORDER[k]: collect(k) for k in range(NX)}
    total = pltpu.roll(jnp.concatenate([parts[d] for d in range(NX)], axis=1), x * CHUNK, 1)
    spread(0, dot(total - shift, T[0], precision=HIGH).astype(BF16))
    pass_on(1)
    finish(1)
    pass_on(0)
    finish(0)
    for cp in sent:
        cp.wait_send()


ROWS = 1024


def apply_shift(HT, Y, E, out):
    rows = pl.ds(pl.multiple_of(pl.program_id(0) * ROWS, ROWS), ROWS)
    out[...] = (E[rows, :].astype(F32) - dot(HT[rows, :], Y[...])).astype(BF16)


def local(eigvecs, panels, tfactors, offsets):
    hbm = pl.BlockSpec(memory_space=pltpu.HBM)
    dma = pltpu.SemaphoreType.DMA
    HT, Y, E = pl.pallas_call(
        gather_and_reduce,
        out_shape=[
            pltpu.VMEM((RD, 2 * NB), BF16),
            pltpu.VMEM((2 * NB, KD), BF16),
            pltpu.VMEM((RD, KD), BF16),
        ],
        in_specs=[hbm] * 4,
        out_specs=[pl.BlockSpec(memory_space=pltpu.VMEM)] * 3,
        scratch_shapes=[
            pltpu.VMEM((2, SLOTS, OWN, RD), BF16),
            pltpu.SMEM((2,), jnp.int32),
            pltpu.VMEM((2, OWN, RD), BF16),
            pltpu.VMEM((2, NB, NB), F32),
            pltpu.VMEM((2, NB, NB), F32),
            pltpu.VMEM((NB, OWN), F32),
            pltpu.VMEM((NB, KD), F32),
            pltpu.VMEM((NB, KH), F32),
            pltpu.VMEM((4, 64, NB), F32),
            pltpu.VMEM((NZ, 4, 8, NB), F32),
            pltpu.VMEM((NX, CHUNK, KD), F32),
            pltpu.VMEM((NX, CHUNK, KH), F32),
            pltpu.VMEM((NX, 64, 128), F32),
            pltpu.VMEM((NX, NZ, 8, 128), F32),
            pltpu.VMEM((16, OWN, NB), F32),
            pltpu.VMEM((SLOTS, OWN, NB), F32),
            pltpu.VMEM((2, 16, 32, NB), BF16),
            dma((4,)),
            dma((2, 20)), dma((2, 20)), dma((2, 20)), dma((2, 20)),
            dma((NX + 1,)), dma((NX + 1,)),
            dma((NX + 1, NZ)), dma((NX + 1, NZ)),
            dma((16,)), dma((16,)), dma((16,)), dma((16,)),
            dma((2, NZ)), dma((2, NZ)),
            dma((2, NZ)), dma((2, NZ)),
        ],
        compiler_params=pltpu.CompilerParams(
            collective_id=0, has_side_effects=True, vmem_limit_bytes=40 * 1024 * 1024
        ),
        name="gather_and_reduce",
    )(*(pltpu.with_memory_space_constraint(v, pltpu.HBM) for v in (offsets, panels, eigvecs, tfactors)))
    whole = pl.BlockSpec(memory_space=pltpu.VMEM)
    return pl.pallas_call(
        apply_shift,
        grid=(RD // ROWS,),
        out_shape=jax.ShapeDtypeStruct((RD, KD), BF16),
        in_specs=[whole, whole, whole],
        out_specs=pl.BlockSpec((ROWS, KD), lambda i: (i, 0)),
        compiler_params=pltpu.CompilerParams(vmem_limit_bytes=40 * 1024 * 1024),
        name="apply_shift",
    )(HT, Y, E)


def solution(mesh):
    return jax.shard_map(
        local,
        mesh=mesh,
        in_specs=(P("row", "col"), P(None, "col", "row"), P(), P()),
        out_specs=P("row", "col"),
        check_vma=False,
    )
```

```python
import jax
import jax.numpy as jnp
from jax import lax
from jax.experimental import pallas as pl
from jax.experimental.pallas import tpu as pltpu
from jax.sharding import PartitionSpec as P

MESH = pl.DeviceIdType.MESH
F32 = jnp.float32
BF16 = jnp.bfloat16
HIGH = lax.Precision.HIGHEST

NB = 128
RD = 6144
KD = 512
KH = KD // 2
NX = 4
NZ = 8
OWN = 8
SLOTS = NX * NX
HALF = RD // 2
QUART = RD // 4
NEAR_A = (0, 1, 4, 5, 6, 7, 10, 11, 12, 13, 14, 15, 18, 19)
CHUNK = NX * OWN
NEAR = (0, 1, 3)


def dot(a, b, dims=((1,), (0,)), precision=None):
    return lax.dot_general(a, b, (dims, ((), ())), precision=precision, preferred_element_type=F32)


def by_place(a):
    return jnp.concatenate([a[(sy * NX + sx) * OWN :][:OWN, :] for sx in range(NX) for sy in range(NX)], axis=0)


def gather_and_reduce(
    offsets, panels, eig, tf, HT, Y, E,
    H, obuf, pbuf, tfbuf, T, ct, w1, c1, x1, z1, wn, cn, xn, zn, wf, cf, xf, zf, crow, C, ybuf,
    local_sem, a_send, a_recv, b_send, b_recv,
    w_send, w_recv, z_send, z_recv, g_send, g_recv, c_send, c_recv, y_send, y_recv, f_send, f_recv,
):
    col = lax.axis_index("col")
    row = lax.axis_index("row")
    x, y = col % NX, col // NX
    z, core = row // 2, row % 2

    def at_x(d):
        return {"col": y * NX + (x + d) % NX}

    def at_y(d):
        return {"col": ((y + d) % NX) * NX + x}

    def at_z(d):
        return {"row": ((z + d) % NZ) * 2 + core}

    sibling = {"row": z * 2 + (1 - core)}

    load_panels = pltpu.make_async_copy(panels, pbuf, local_sem.at[0])
    load_offsets = pltpu.make_async_copy(offsets, obuf, local_sem.at[3])
    load_tf = pltpu.make_async_copy(tf, tfbuf, local_sem.at[1])
    load_eig = pltpu.make_async_copy(eig, E, local_sem.at[2])
    load_panels.start()
    load_offsets.start()
    load_tf.start()
    load_eig.start()

    barrier = pltpu.get_barrier_semaphore()
    for d in range(1, 16):
        pl.semaphore_signal(barrier, inc=1, device_id={"col": (col + d) % 16}, device_id_type=MESH)
        pl.semaphore_signal(barrier, inc=1, device_id={"row": (row + d) % 16}, device_id_type=MESH)

    slot = x * NX + y
    load_panels.wait()
    load_offsets.wait()
    step = 512
    for p in range(2):
        pivot = obuf[p] + col * OWN + lax.broadcasted_iota(jnp.int32, (OWN, step), 0)
        for s in range(0, RD, step):
            position = row * RD + s + lax.broadcasted_iota(jnp.int32, (OWN, step), 1)
            v = pbuf[p, :, s : s + step].astype(F32)
            v = jnp.where(position > pivot, v, jnp.where(position == pivot, 1.0, 0.0))
            H[p, slot, :, s : s + step] = v.astype(BF16)

    pl.semaphore_wait(barrier, 30)

    def part(p, dx, dy, lo, n):
        return H.at[p, ((x + dx) % NX) * NX + (y + dy) % NX, :, lo : lo + n]

    sent = []

    def send(src, dst, send_sem, recv_sem, dev):
        cp = pltpu.make_async_remote_copy(src, dst, send_sem, recv_sem, device_id=dev, device_id_type=MESH)
        cp.start()
        sent.append(cp)

    def recv(ref, send_sem, recv_sem):
        pltpu.make_async_remote_copy(
            ref, ref, send_sem, recv_sem, device_id=sibling, device_id_type=MESH
        ).wait_recv()

    class Half:
        def __init__(self, p, lo, sems, first, second, turn):
            self.p, self.lo, self.sems = p, lo, sems
            self.first, self.second, self.turn = first, second, turn
            self.got = set()

        def ref(self, d1, d2, piece=None):
            lo, n = (self.lo, HALF) if piece is None else (self.lo + piece * QUART, QUART)
            return part(self.p, d2, d1, lo, n) if self.turn else part(self.p, d1, d2, lo, n)

        def put(self, ref, i, dev):
            send(ref, ref, self.sems[0].at[self.p, i], self.sems[1].at[self.p, i], dev)

        def get(self, i):
            if i in self.got:
                return
            self.got.add(i)
            if i < 2:
                ref = self.ref((-1, 1)[i], 0)
            elif i < 4:
                ref = self.ref(2, 0, i - 2)
            elif i < 12:
                ref = self.ref((i - 4) // 2, (-1, 1)[i % 2])
            else:
                ref = self.ref((i - 12) // 2, 2, i % 2)
            recv(ref, self.sems[0].at[self.p, i], self.sems[1].at[self.p, i])

        def line(self, d):
            self.put(self.ref(d, 0), 4 + 2 * d, self.second(1))
            self.put(self.ref(d, 0), 5 + 2 * d, self.second(-1))

        def own(self):
            self.put(self.ref(0, 0), 0, self.first(1))
            self.put(self.ref(0, 0), 1, self.first(-1))

        def own_line(self):
            self.line(0)

        def up(self):
            self.get(0)
            self.put(self.ref(-1, 0, 0), 2, self.first(1))

        def down(self):
            self.get(1)
            self.put(self.ref(1, 0, 1), 3, self.first(-1))

        def low_line(self):
            self.get(0)
            self.line(3)

        def high_line(self):
            self.get(1)
            self.line(1)

        def far_line(self):
            self.get(2)
            self.get(3)
            self.line(2)

        def up_line(self, d):
            self.get(4 + 2 * d)
            self.put(self.ref(d, -1, 0), 12 + 2 * d, self.second(1))

        def down_line(self, d):
            self.get(5 + 2 * d)
            self.put(self.ref(d, 1, 1), 13 + 2 * d, self.second(-1))

        def need(self, keys):
            for i in keys:
                self.get(i)

    halves = {
        p: (
            Half(p, 0, (a_send, a_recv), at_x, at_y, False),
            Half(p, HALF, (b_send, b_recv), at_y, at_x, True),
        )
        for p in range(2)
    }
    a0, b0 = halves[0]
    a1, b1 = halves[1]

    theirs = pl.ds(pl.multiple_of((1 - core) * KH, KH), KH)
    mine = pl.ds(pl.multiple_of(core * KH, KH), KH)

    first_one = []

    def products_one(half, lo, n):
        half.need(range(20))
        k = slice(lo, lo + n)
        h = H[1, :, :, k].reshape(NB, n)
        s = dot(h, E[k, :])
        c = dot(h, H[0, slot, :, k], ((1,), (1,)))
        w1[...] = s + w1[...] if first_one else s
        ct[...] = c + ct[...] if first_one else c
        first_one.append(lo)

    def swap_one():
        send(w1.at[:, theirs], c1, w_send.at[2], w_recv.at[2], sibling)
        crow[0] = ct[...].T
        for d in range(1, 16):
            send(crow.at[0], crow.at[d], g_send.at[d], g_recv.at[d], {"row": (row + d) % 16})

    def scatter_one():
        recv(c1, w_send.at[2], w_recv.at[2])
        x1[...] = (w1[:, mine] + c1[...]).T.reshape(4, 64, NB)
        for d in (4, 3, 5, 2, 6, 1, 7):
            r = pl.multiple_of(((z + d) % NZ) * 8, 8)
            send(x1.at[:, pl.ds(r, 8), :], z1.at[d], z_send.at[2, d], z_recv.at[2, d], at_z(d))

    def collect_one():
        total = x1[:, pl.ds(pl.multiple_of(z * 8, 8), 8), :]
        for d in range(1, NZ):
            recv(z1.at[d], z_send.at[2, d], z_recv.at[2, d])
            total = total + z1[d]
        return total.reshape(32, NB)

    first_near = []

    def near(half, keys, lo, n):
        half.need(keys)
        k = slice(lo, lo + n)
        h = [H[0, pl.ds(((x + d) % NX) * NX, NX), :, k].reshape(CHUNK, n) for d in NEAR]
        s = dot(jnp.concatenate(h, axis=0), E[k, :])
        wn[...] = s + wn[...] if first_near else s
        first_near.append(lo)

    def swap_near():
        send(wn.at[:, theirs], cn, w_send.at[0], w_recv.at[0], sibling)

    def scatter_near():
        recv(cn, w_send.at[0], w_recv.at[0])
        s = jnp.concatenate([wn[:, mine] + cn[...], jnp.zeros((CHUNK, KH), F32)], axis=0)
        xn[...] = s.T.reshape(4, 64, NB)
        for d in (4, 3, 5, 2, 6, 1, 7):
            r = pl.multiple_of(((z + d) % NZ) * 8, 8)
            send(xn.at[:, pl.ds(r, 8), :], zn.at[d], z_send.at[0, d], z_recv.at[0, d], at_z(d))

    def collect_near():
        total = xn[:, pl.ds(pl.multiple_of(z * 8, 8), 8), :]
        for d in range(1, NZ):
            recv(zn.at[d], z_send.at[0, d], z_recv.at[0, d])
            total = total + zn[d]
        return total.reshape(32, NB)[:, : 3 * CHUNK]

    first_far = []

    def far(half, keys, lo, n):
        half.need(keys)
        k = slice(lo, lo + n)
        s = dot(H[0, pl.ds(((x + 2) % NX) * NX, NX), :, k].reshape(CHUNK, n), E[k, :])
        wf[...] = s + wf[...] if first_far else s
        first_far.append(lo)

    def swap_far():
        send(wf.at[:, theirs], cf, w_send.at[1], w_recv.at[1], sibling)

    def scatter_far():
        recv(cf, w_send.at[1], w_recv.at[1])
        s = wf[:, mine] + cf[...]
        xf[...] = jnp.concatenate([s[:, g * 64 : g * 64 + 64] for g in range(4)], axis=0).T
        for d in (4, 3, 5, 2, 6, 1, 7):
            r = pl.multiple_of(((z + d) % NZ) * 8, 8)
            send(xf.at[pl.ds(r, 8), :], zf.at[d], z_send.at[1, d], z_recv.at[1, d], at_z(d))

    def collect_far():
        total = xf[pl.ds(pl.multiple_of(z * 8, 8), 8), :]
        for d in range(1, NZ):
            recv(zf.at[d], z_send.at[1, d], z_recv.at[1, d])
            total = total + zf[d]
        return jnp.concatenate([total[:, g * CHUNK : (g + 1) * CHUNK] for g in range(4)], axis=0)

    def cross_sum():
        total = crow[0]
        for d in range(1, 16):
            recv(crow.at[d], g_send.at[d], g_recv.at[d])
            total = total + crow[d]
        C[slot] = total
        for d in range(1, 16):
            send(C.at[slot], C.at[slot], c_send.at[d], c_recv.at[d], {"col": (col + d) % 16})

    def cross_recv():
        for d in range(1, 16):
            o = (col + 16 - d) % 16
            recv(C.at[(o % NX) * NX + o // NX], c_send.at[d], c_recv.at[d])
        return C[...].reshape(NB, NB)

    def spread(p, value):
        ref = ybuf.at[p, core * NZ + z]
        ybuf[p, core * NZ + z] = value
        for d in (4, 3, 5, 2, 6, 1, 7):
            send(ref, ref, y_send.at[p, d], y_recv.at[p, d], at_z(d))
        send(ref, ref, f_send.at[p, 0], f_recv.at[p, 0], sibling)

    def pass_on(p):
        for d in (1, 7, 2, 6, 3, 5, 4):
            ref = ybuf.at[p, core * NZ + (z + NZ - d) % NZ]
            recv(ref, y_send.at[p, d], y_recv.at[p, d])
            send(ref, ref, f_send.at[p, d], f_recv.at[p, d], sibling)

    def place(p, c):
        v = [ybuf[p, c * NZ + i].astype(F32) for i in range(NZ)]
        v = jnp.concatenate([v[i][g * 8 : g * 8 + 8, :] for g in range(4) for i in range(NZ)], axis=0)
        Y[p * NB : (p + 1) * NB, pl.ds(pl.multiple_of(c * KH, KH), KH)] = v.T.astype(BF16)

    def finish(p):
        place(p, core)
        for d in range(NZ):
            recv(ybuf.at[p, (1 - core) * NZ + (z + NZ - d) % NZ], f_send.at[p, d], f_recv.at[p, d])
        place(p, 1 - core)

    def turn(p):
        for r in range(0, RD, 512):
            HT[r : r + 512, p * NB : (p + 1) * NB] = H[p, :, :, r : r + 512].reshape(NB, 512).T

    def upper_factors():
        load_tf.wait()
        tri = lax.broadcasted_iota(jnp.int32, (NB, NB), 0) <= lax.broadcasted_iota(jnp.int32, (NB, NB), 1)
        for p in range(2):
            T[p] = by_place(by_place(jnp.where(tri, tfbuf[p], 0.0)).T)

    b1.own()
    b0.own()
    a1.own()
    a0.own()
    b1.own_line()
    a0.own_line()
    upper_factors()
    b1.high_line()
    b1.down()
    b1.up()
    a1.up()
    a1.own_line()
    a1.down()
    a0.up()
    a1.high_line()
    b1.low_line()
    b0.down()
    b1.down_line(0)
    b0.up()
    a1.low_line()
    b1.far_line()
    b0.high_line()
    a1.far_line()
    b1.up_line(0)
    a0.low_line()
    a0.high_line()
    a1.down_line(0)
    b1.up_line(1)
    a0.down()
    b1.down_line(1)
    b1.up_line(3)
    b1.down_line(2)
    b1.up_line(2)
    a0.down_line(0)
    a1.up_line(1)
    b1.down_line(3)
    a1.down_line(3)
    b0.low_line()
    a1.up_line(0)
    a1.down_line(1)
    a1.down_line(2)
    a1.up_line(3)
    b0.own_line()
    b0.far_line()
    b0.down_line(1)
    b0.up_line(1)
    a1.up_line(2)
    a0.far_line()
    a0.up_line(0)
    a0.down_line(1)
    a0.down_line(3)
    load_eig.wait()
    products_one(b1, HALF + QUART, QUART)
    products_one(b1, HALF, QUART)
    b0.down_line(3)
    b0.up_line(0)
    b0.up_line(3)
    a0.up_line(3)
    a0.up_line(1)
    b0.down_line(0)
    products_one(a1, 0, QUART)
    b0.down_line(2)
    b0.up_line(2)
    a0.down_line(2)
    products_one(a1, QUART, QUART)
    a0.up_line(2)
    near(b0, range(12), HALF, QUART)
    swap_one()
    near(a0, NEAR_A, QUART, QUART)
    near(a0, NEAR_A, 0, QUART)
    near(b0, range(12), HALF + QUART, QUART)
    swap_near()
    scatter_one()
    far(a0, range(20), 0, HALF)
    scatter_near()
    far(b0, range(20), HALF, HALF)
    swap_far()
    cross_sum()
    scatter_far()
    y1 = dot(collect_one(), T[1], precision=HIGH).astype(BF16)
    spread(1, y1)
    turn(1)
    turn(0)
    cross = cross_recv()
    shift = dot(y1.astype(F32), cross, ((1,), (1,)), precision=HIGH)
    near_sum = collect_near()
    total = [near_sum[:, : 2 * CHUNK], collect_far(), near_sum[:, 2 * CHUNK :]]
    total = pltpu.roll(jnp.concatenate(total, axis=1), x * CHUNK, 1)
    spread(0, dot(total - shift, T[0], precision=HIGH).astype(BF16))
    pass_on(1)
    finish(1)
    pass_on(0)
    finish(0)
    for cp in sent:
        cp.wait_send()


ROWS = 512


def apply_shift(HT, Y, E, out, done, sems):
    copies = []
    for i in range(RD // ROWS):
        rows = slice(i * ROWS, (i + 1) * ROWS)
        done[rows, :] = (E[rows, :].astype(F32) - dot(HT[rows, :], Y[...])).astype(BF16)
        copies.append(pltpu.make_async_copy(done.at[rows, :], out.at[rows, :], sems.at[i]))
        copies[-1].start()
    for cp in copies:
        cp.wait()


def local(eigvecs, panels, tfactors, offsets):
    hbm = pl.BlockSpec(memory_space=pltpu.HBM)
    dma = pltpu.SemaphoreType.DMA
    HT, Y, E = pl.pallas_call(
        gather_and_reduce,
        out_shape=[
            pltpu.VMEM((RD, 2 * NB), BF16),
            pltpu.VMEM((2 * NB, KD), BF16),
            pltpu.VMEM((RD, KD), BF16),
        ],
        in_specs=[hbm] * 4,
        out_specs=[pl.BlockSpec(memory_space=pltpu.VMEM)] * 3,
        scratch_shapes=[
            pltpu.VMEM((2, SLOTS, OWN, RD), BF16),
            pltpu.SMEM((2,), jnp.int32),
            pltpu.VMEM((2, OWN, RD), BF16),
            pltpu.VMEM((2, NB, NB), F32),
            pltpu.VMEM((2, NB, NB), F32),
            pltpu.VMEM((NB, OWN), F32),
            pltpu.VMEM((NB, KD), F32),
            pltpu.VMEM((NB, KH), F32),
            pltpu.VMEM((4, 64, NB), F32),
            pltpu.VMEM((NZ, 4, 8, NB), F32),
            pltpu.VMEM((3 * CHUNK, KD), F32),
            pltpu.VMEM((3 * CHUNK, KH), F32),
            pltpu.VMEM((4, 64, NB), F32),
            pltpu.VMEM((NZ, 4, 8, NB), F32),
            pltpu.VMEM((CHUNK, KD), F32),
            pltpu.VMEM((CHUNK, KH), F32),
            pltpu.VMEM((64, 128), F32),
            pltpu.VMEM((NZ, 8, 128), F32),
            pltpu.VMEM((16, OWN, NB), F32),
            pltpu.VMEM((SLOTS, OWN, NB), F32),
            pltpu.VMEM((2, 16, 32, NB), BF16),
            dma((4,)),
            dma((2, 20)), dma((2, 20)), dma((2, 20)), dma((2, 20)),
            dma((3,)), dma((3,)),
            dma((3, NZ)), dma((3, NZ)),
            dma((16,)), dma((16,)), dma((16,)), dma((16,)),
            dma((2, NZ)), dma((2, NZ)),
            dma((2, NZ)), dma((2, NZ)),
        ],
        compiler_params=pltpu.CompilerParams(
            collective_id=0, has_side_effects=True, vmem_limit_bytes=40 * 1024 * 1024
        ),
        name="gather_and_reduce",
    )(*(pltpu.with_memory_space_constraint(v, pltpu.HBM) for v in (offsets, panels, eigvecs, tfactors)))
    whole = pl.BlockSpec(memory_space=pltpu.VMEM)
    return pl.pallas_call(
        apply_shift,
        out_shape=jax.ShapeDtypeStruct((RD, KD), BF16),
        in_specs=[whole, whole, whole],
        out_specs=hbm,
        scratch_shapes=[pltpu.VMEM((RD, KD), BF16), dma((RD // ROWS,))],
        compiler_params=pltpu.CompilerParams(vmem_limit_bytes=40 * 1024 * 1024),
        name="apply_shift",
    )(HT, Y, E)


def solution(mesh):
    return jax.shard_map(
        local,
        mesh=mesh,
        in_specs=(P("row", "col"), P(None, "col", "row"), P(), P()),
        out_specs=P("row", "col"),
        check_vma=False,
    )
```

```python
import jax
import jax.numpy as jnp
from jax import lax
from jax.experimental import pallas as pl
from jax.experimental.pallas import tpu as pltpu
from jax.sharding import PartitionSpec as P

MESH = pl.DeviceIdType.MESH
F32 = jnp.float32
BF16 = jnp.bfloat16
HIGH = lax.Precision.HIGHEST

NB = 128
RD = 6144
KD = 512
KH = KD // 2
NX = 4
NZ = 8
OWN = 8
SLOTS = NX * NX
HALF = RD // 2
QUART = RD // 4


def dot(a, b, dims=((1,), (0,)), precision=None):
    return lax.dot_general(a, b, (dims, ((), ())), precision=precision, preferred_element_type=F32)


def by_place(a):
    return jnp.concatenate([a[(sy * NX + sx) * OWN :][:OWN, :] for sx in range(NX) for sy in range(NX)], axis=0)


def gather_and_reduce(
    offsets, panels, eig, tf, HT, Y, E,
    H, obuf, pbuf, tfbuf, T, ct, w1, c1, x1, z1, w0, c0, x0, z0, crow, C, ybuf,
    local_sem, a_send, a_recv, b_send, b_recv,
    w_send, w_recv, z_send, z_recv, g_send, g_recv, c_send, c_recv, y_send, y_recv, f_send, f_recv,
):
    col = lax.axis_index("col")
    row = lax.axis_index("row")
    x, y = col % NX, col // NX
    z, core = row // 2, row % 2

    def at_x(d):
        return {"col": y * NX + (x + d) % NX}

    def at_y(d):
        return {"col": ((y + d) % NX) * NX + x}

    def at_z(d):
        return {"row": ((z + d) % NZ) * 2 + core}

    sibling = {"row": z * 2 + (1 - core)}

    load_panels = pltpu.make_async_copy(panels, pbuf, local_sem.at[0])
    load_offsets = pltpu.make_async_copy(offsets, obuf, local_sem.at[3])
    load_tf = pltpu.make_async_copy(tf, tfbuf, local_sem.at[1])
    load_eig = pltpu.make_async_copy(eig, E, local_sem.at[2])
    load_panels.start()
    load_offsets.start()
    load_tf.start()
    load_eig.start()

    barrier = pltpu.get_barrier_semaphore()
    for d in range(1, 16):
        pl.semaphore_signal(barrier, inc=1, device_id={"col": (col + d) % 16}, device_id_type=MESH)
        pl.semaphore_signal(barrier, inc=1, device_id={"row": (row + d) % 16}, device_id_type=MESH)

    slot = x * NX + y
    load_panels.wait()
    load_offsets.wait()
    step = 512
    for p in range(2):
        pivot = obuf[p] + col * OWN + lax.broadcasted_iota(jnp.int32, (OWN, step), 0)
        for s in range(0, RD, step):
            position = row * RD + s + lax.broadcasted_iota(jnp.int32, (OWN, step), 1)
            v = pbuf[p, :, s : s + step].astype(F32)
            v = jnp.where(position > pivot, v, jnp.where(position == pivot, 1.0, 0.0))
            H[p, slot, :, s : s + step] = v.astype(BF16)

    pl.semaphore_wait(barrier, 30)

    def part(p, dx, dy, lo, n):
        return H.at[p, ((x + dx) % NX) * NX + (y + dy) % NX, :, lo : lo + n]

    sent = []

    def send(src, dst, send_sem, recv_sem, dev):
        cp = pltpu.make_async_remote_copy(src, dst, send_sem, recv_sem, device_id=dev, device_id_type=MESH)
        cp.start()
        sent.append(cp)

    def settle():
        for cp in sent:
            cp.wait_send()
        sent.clear()

    def recv(ref, send_sem, recv_sem):
        pltpu.make_async_remote_copy(
            ref, ref, send_sem, recv_sem, device_id=sibling, device_id_type=MESH
        ).wait_recv()

    class Half:
        def __init__(self, p, lo, sems, first, second, turn):
            self.p, self.lo, self.sems = p, lo, sems
            self.first, self.second, self.turn = first, second, turn
            self.got = set()

        def ref(self, d1, d2, piece=None):
            lo, n = (self.lo, HALF) if piece is None else (self.lo + piece * QUART, QUART)
            return part(self.p, d2, d1, lo, n) if self.turn else part(self.p, d1, d2, lo, n)

        def put(self, ref, i, dev):
            send(ref, ref, self.sems[0].at[self.p, i], self.sems[1].at[self.p, i], dev)

        def get(self, i):
            if i in self.got:
                return
            self.got.add(i)
            if i < 2:
                ref = self.ref((-1, 1)[i], 0)
            elif i < 4:
                ref = self.ref(2, 0, i - 2)
            elif i < 12:
                ref = self.ref((i - 4) // 2, (-1, 1)[i % 2])
            else:
                ref = self.ref((i - 12) // 2, 2, i % 2)
            recv(ref, self.sems[0].at[self.p, i], self.sems[1].at[self.p, i])

        def line(self, d):
            self.put(self.ref(d, 0), 4 + 2 * d, self.second(1))
            self.put(self.ref(d, 0), 5 + 2 * d, self.second(-1))

        def own(self):
            self.put(self.ref(0, 0), 0, self.first(1))
            self.put(self.ref(0, 0), 1, self.first(-1))

        def own_line(self):
            self.line(0)

        def up(self):
            self.get(0)
            self.put(self.ref(-1, 0, 0), 2, self.first(1))

        def down(self):
            self.get(1)
            self.put(self.ref(1, 0, 1), 3, self.first(-1))

        def low_line(self):
            self.get(0)
            self.line(3)

        def high_line(self):
            self.get(1)
            self.line(1)

        def far_line(self):
            self.get(2)
            self.get(3)
            self.line(2)

        def up_line(self, d):
            self.get(4 + 2 * d)
            self.put(self.ref(d, -1, 0), 12 + 2 * d, self.second(1))

        def down_line(self, d):
            self.get(5 + 2 * d)
            self.put(self.ref(d, 1, 1), 13 + 2 * d, self.second(-1))

        def need(self, keys):
            for i in keys:
                self.get(i)

    halves = {
        p: (
            Half(p, 0, (a_send, a_recv), at_x, at_y, False),
            Half(p, HALF, (b_send, b_recv), at_y, at_x, True),
        )
        for p in range(2)
    }
    a0, b0 = halves[0]
    a1, b1 = halves[1]

    theirs = pl.ds(pl.multiple_of((1 - core) * KH, KH), KH)
    mine = pl.ds(pl.multiple_of(core * KH, KH), KH)

    first_one = []

    def products_one(half, lo, n):
        half.need(range(20))
        k = slice(lo, lo + n)
        h = H[1, :, :, k].reshape(NB, n)
        s = dot(h, E[k, :])
        c = dot(h, H[0, slot, :, k], ((1,), (1,)))
        w1[...] = s + w1[...] if first_one else s
        ct[...] = c + ct[...] if first_one else c
        first_one.append(lo)

    def send_cross():
        crow[0] = ct[...].T
        for d in range(1, 16):
            send(crow.at[0], crow.at[d], g_send.at[d], g_recv.at[d], {"row": (row + d) % 16})

    first_zero = []

    def products_zero(half, lo, n):
        half.need(range(20))
        k = slice(lo, lo + n)
        w = dot(H[0, :, :, k].reshape(NB, n), E[k, :])
        w0[...] = w + w0[...] if first_zero else w
        first_zero.append(lo)

    def swap(i, w, c):
        send(w.at[:, theirs], c, w_send.at[i], w_recv.at[i], sibling)

    def scatter(i, w, c, xs, zs):
        recv(c, w_send.at[i], w_recv.at[i])
        s = (w[:, mine] + c[...]).T.reshape(4, NZ, 8, NB)
        for g in range(4):
            xs[:, g] = s[g]
        for d in (4, 3, 5, 2, 6, 1, 7):
            send(xs.at[(z + d) % NZ], zs.at[d], z_send.at[i, d], z_recv.at[i, d], at_z(d))

    def collect(i, xs, zs):
        total = xs[z]
        for d in range(1, NZ):
            recv(zs.at[d], z_send.at[i, d], z_recv.at[i, d])
            total = total + zs[d]
        return total.reshape(32, NB)

    def cross_sum():
        total = crow[0]
        for d in range(1, 16):
            recv(crow.at[d], g_send.at[d], g_recv.at[d])
            total = total + crow[d]
        C[slot] = total
        for d in range(1, 16):
            send(C.at[slot], C.at[slot], c_send.at[d], c_recv.at[d], {"col": (col + d) % 16})

    def cross_recv():
        for d in range(1, 16):
            o = (col + 16 - d) % 16
            recv(C.at[(o % NX) * NX + o // NX], c_send.at[d], c_recv.at[d])
        return C[...].reshape(NB, NB)

    def spread(p, value):
        ref = ybuf.at[p, core * NZ + z]
        ybuf[p, core * NZ + z] = value
        for d in (4, 3, 5, 2, 6, 1, 7):
            send(ref, ref, y_send.at[p, d], y_recv.at[p, d], at_z(d))
        send(ref, ref, f_send.at[p, 0], f_recv.at[p, 0], sibling)

    def pass_on(p):
        for d in (1, 7, 2, 6, 3, 5, 4):
            ref = ybuf.at[p, core * NZ + (z + NZ - d) % NZ]
            recv(ref, y_send.at[p, d], y_recv.at[p, d])
            send(ref, ref, f_send.at[p, d], f_recv.at[p, d], sibling)

    def place(p, c):
        v = [ybuf[p, c * NZ + i].astype(F32) for i in range(NZ)]
        v = jnp.concatenate([v[i][g * 8 : g * 8 + 8, :] for g in range(4) for i in range(NZ)], axis=0)
        Y[p * NB : (p + 1) * NB, pl.ds(pl.multiple_of(c * KH, KH), KH)] = v.T.astype(BF16)

    def finish(p):
        place(p, core)
        for d in range(NZ):
            recv(ybuf.at[p, (1 - core) * NZ + (z + NZ - d) % NZ], f_send.at[p, d], f_recv.at[p, d])
        place(p, 1 - core)

    def turn(p):
        for r in range(0, RD, 512):
            HT[r : r + 512, p * NB : (p + 1) * NB] = H[p, :, :, r : r + 512].reshape(NB, 512).T

    def upper_factors():
        load_tf.wait()
        tri = lax.broadcasted_iota(jnp.int32, (NB, NB), 0) <= lax.broadcasted_iota(jnp.int32, (NB, NB), 1)
        for p in range(2):
            T[p] = by_place(by_place(jnp.where(tri, tfbuf[p], 0.0)).T)

    b1.own()
    a1.own_line()
    a1.own()
    b0.own()
    b0.own_line()
    a0.own()
    a0.own_line()
    upper_factors()
    a1.up()
    a1.down()
    b1.up()
    a1.low_line()
    b1.high_line()
    b1.down()
    b1.own_line()
    a1.high_line()
    b0.low_line()
    b0.up()
    a0.up()
    a1.far_line()
    a1.up_line(0)
    a1.down_line(0)
    a0.down()
    b1.low_line()
    b1.far_line()
    a0.high_line()
    b0.down()
    a0.down_line(0)
    a1.down_line(1)
    b1.up_line(0)
    a1.down_line(3)
    a1.up_line(1)
    b1.down_line(1)
    b0.high_line()
    b1.down_line(0)
    a1.up_line(2)
    b1.up_line(3)
    b0.up_line(0)
    a1.down_line(2)
    a0.up_line(0)
    a1.up_line(3)
    a0.low_line()
    b1.up_line(1)
    a0.far_line()
    b1.down_line(2)
    b0.far_line()
    a0.down_line(1)
    b1.down_line(3)
    b1.up_line(2)
    b0.down_line(1)
    b0.down_line(0)
    b0.up_line(3)
    b0.up_line(1)
    b0.down_line(3)
    a0.up_line(1)
    load_eig.wait()
    products_one(a1, 0, HALF)
    b0.down_line(2)
    b0.up_line(2)
    a0.down_line(3)
    a0.up_line(3)
    a0.up_line(2)
    a0.down_line(2)
    products_one(b1, HALF, HALF)
    send_cross()
    swap(1, w1, c1)
    products_zero(b0, HALF, HALF)
    scatter(1, w1, c1, x1, z1)
    products_zero(a0, 0, HALF)
    swap(0, w0, c0)
    scatter(0, w0, c0, x0, z0)
    cross_sum()
    y1 = dot(collect(1, x1, z1), T[1], precision=HIGH).astype(BF16)
    spread(1, y1)
    turn(1)
    turn(0)
    cross = cross_recv()
    shift = dot(y1.astype(F32), cross, ((1,), (1,)), precision=HIGH)
    total = collect(0, x0, z0)
    spread(0, dot(total - shift, T[0], precision=HIGH).astype(BF16))
    pass_on(1)
    finish(1)
    settle()
    pass_on(0)
    finish(0)
    settle()


ROWS = 512


def apply_shift(HT, Y, E, out, done, sems):
    copies = []
    for i in range(RD // ROWS):
        rows = slice(i * ROWS, (i + 1) * ROWS)
        done[rows, :] = (E[rows, :].astype(F32) - dot(HT[rows, :], Y[...])).astype(BF16)
        copies.append(pltpu.make_async_copy(done.at[rows, :], out.at[rows, :], sems.at[i]))
        copies[-1].start()
    for cp in copies:
        cp.wait()


def local(eigvecs, panels, tfactors, offsets):
    hbm = pl.BlockSpec(memory_space=pltpu.HBM)
    dma = pltpu.SemaphoreType.DMA
    HT, Y, E = pl.pallas_call(
        gather_and_reduce,
        out_shape=[
            pltpu.VMEM((RD, 2 * NB), BF16),
            pltpu.VMEM((2 * NB, KD), BF16),
            pltpu.VMEM((RD, KD), BF16),
        ],
        in_specs=[hbm] * 4,
        out_specs=[pl.BlockSpec(memory_space=pltpu.VMEM)] * 3,
        scratch_shapes=[
            pltpu.VMEM((2, SLOTS, OWN, RD), BF16),
            pltpu.SMEM((2,), jnp.int32),
            pltpu.VMEM((2, OWN, RD), BF16),
            pltpu.VMEM((2, NB, NB), F32),
            pltpu.VMEM((2, NB, NB), F32),
            pltpu.VMEM((NB, OWN), F32),
            pltpu.VMEM((NB, KD), F32),
            pltpu.VMEM((NB, KH), F32),
            pltpu.VMEM((NZ, 4, 8, NB), F32),
            pltpu.VMEM((NZ, 4, 8, NB), F32),
            pltpu.VMEM((NB, KD), F32),
            pltpu.VMEM((NB, KH), F32),
            pltpu.VMEM((NZ, 4, 8, NB), F32),
            pltpu.VMEM((NZ, 4, 8, NB), F32),
            pltpu.VMEM((16, OWN, NB), F32),
            pltpu.VMEM((SLOTS, OWN, NB), F32),
            pltpu.VMEM((2, 16, 32, NB), BF16),
            dma((4,)),
            dma((2, 20)), dma((2, 20)), dma((2, 20)), dma((2, 20)),
            dma((2,)), dma((2,)),
            dma((2, NZ)), dma((2, NZ)),
            dma((16,)), dma((16,)), dma((16,)), dma((16,)),
            dma((2, NZ)), dma((2, NZ)),
            dma((2, NZ)), dma((2, NZ)),
        ],
        compiler_params=pltpu.CompilerParams(
            collective_id=0, has_side_effects=True, vmem_limit_bytes=40 * 1024 * 1024
        ),
        name="gather_and_reduce",
    )(*(pltpu.with_memory_space_constraint(v, pltpu.HBM) for v in (offsets, panels, eigvecs, tfactors)))
    whole = pl.BlockSpec(memory_space=pltpu.VMEM)
    return pl.pallas_call(
        apply_shift,
        out_shape=jax.ShapeDtypeStruct((RD, KD), BF16),
        in_specs=[whole, whole, whole],
        out_specs=hbm,
        scratch_shapes=[pltpu.VMEM((RD, KD), BF16), dma((RD // ROWS,))],
        compiler_params=pltpu.CompilerParams(vmem_limit_bytes=40 * 1024 * 1024),
        name="apply_shift",
    )(HT, Y, E)


def solution(mesh):
    return jax.shard_map(
        local,
        mesh=mesh,
        in_specs=(P("row", "col"), P(None, "col", "row"), P(), P()),
        out_specs=P("row", "col"),
        check_vma=False,
    )
```

```python
import jax
import jax.numpy as jnp
from jax import lax
from jax.experimental import pallas as pl
from jax.experimental.pallas import tpu as pltpu
from jax.sharding import PartitionSpec as P

MESH = pl.DeviceIdType.MESH
F32 = jnp.float32
BF16 = jnp.bfloat16
HIGH = lax.Precision.HIGHEST

NB = 128
RD = 6144
KD = 512
KH = KD // 2
NX = 4
NZ = 8
OWN = 8
SLOTS = NX * NX
FAR = (4,)
HALF = RD // 2
QUART = RD // 4


def dot(a, b, dims=((1,), (0,)), precision=None):
    return lax.dot_general(a, b, (dims, ((), ())), precision=precision, preferred_element_type=F32)


def by_place(a):
    return jnp.concatenate([a[(sy * NX + sx) * OWN :][:OWN, :] for sx in range(NX) for sy in range(NX)], axis=0)


def gather_and_reduce(
    offsets, panels, eig, tf, HT, Y, E,
    H, obuf, pbuf, tfbuf, T, ct, w1, c1, x1, z1, w0, c0, x0, z0, crow, C, ybuf,
    local_sem, a_send, a_recv, b_send, b_recv,
    w_send, w_recv, z_send, z_recv, g_send, g_recv, c_send, c_recv, y_send, y_recv, f_send, f_recv,
):
    col = lax.axis_index("col")
    row = lax.axis_index("row")
    x, y = col % NX, col // NX
    z, core = row // 2, row % 2

    def at_x(d):
        return {"col": y * NX + (x + d) % NX}

    def at_y(d):
        return {"col": ((y + d) % NX) * NX + x}

    def at_z(d, c=core):
        return {"row": ((z + d) % NZ) * 2 + c}

    sibling = {"row": z * 2 + (1 - core)}

    load_panels = pltpu.make_async_copy(panels, pbuf, local_sem.at[0])
    load_offsets = pltpu.make_async_copy(offsets, obuf, local_sem.at[3])
    load_tf = pltpu.make_async_copy(tf, tfbuf, local_sem.at[1])
    load_eig = pltpu.make_async_copy(eig, E, local_sem.at[2])
    load_panels.start()
    load_offsets.start()
    load_tf.start()
    load_eig.start()

    barrier = pltpu.get_barrier_semaphore()
    for d in range(1, 16):
        pl.semaphore_signal(barrier, inc=1, device_id={"col": (col + d) % 16}, device_id_type=MESH)
        pl.semaphore_signal(barrier, inc=1, device_id={"row": (row + d) % 16}, device_id_type=MESH)

    slot = x * NX + y
    load_panels.wait()
    load_offsets.wait()
    step = 512
    for p in range(2):
        pivot = obuf[p] + col * OWN + lax.broadcasted_iota(jnp.int32, (OWN, step), 0)
        for s in range(0, RD, step):
            position = row * RD + s + lax.broadcasted_iota(jnp.int32, (OWN, step), 1)
            v = pbuf[p, :, s : s + step].astype(F32)
            v = jnp.where(position > pivot, v, jnp.where(position == pivot, 1.0, 0.0))
            H[p, slot, :, s : s + step] = v.astype(BF16)

    pl.semaphore_wait(barrier, 30)

    def part(p, dx, dy, lo, n):
        return H.at[p, ((x + dx) % NX) * NX + (y + dy) % NX, :, lo : lo + n]

    sent = []

    def send(src, dst, send_sem, recv_sem, dev):
        cp = pltpu.make_async_remote_copy(src, dst, send_sem, recv_sem, device_id=dev, device_id_type=MESH)
        cp.start()
        sent.append(cp)

    def settle():
        for cp in sent:
            cp.wait_send()
        sent.clear()

    def recv(ref, send_sem, recv_sem):
        pltpu.make_async_remote_copy(
            ref, ref, send_sem, recv_sem, device_id=sibling, device_id_type=MESH
        ).wait_recv()

    class Half:
        def __init__(self, p, lo, sems, first, second, turn):
            self.p, self.lo, self.sems = p, lo, sems
            self.first, self.second, self.turn = first, second, turn
            self.got = set()

        def ref(self, d1, d2, piece=None):
            lo, n = (self.lo, HALF) if piece is None else (self.lo + piece * QUART, QUART)
            return part(self.p, d2, d1, lo, n) if self.turn else part(self.p, d1, d2, lo, n)

        def put(self, ref, i, dev):
            send(ref, ref, self.sems[0].at[self.p, i], self.sems[1].at[self.p, i], dev)

        def get(self, i):
            if i in self.got:
                return
            self.got.add(i)
            if i < 2:
                ref = self.ref((-1, 1)[i], 0)
            elif i < 4:
                ref = self.ref(2, 0, i - 2)
            elif i < 12:
                ref = self.ref((i - 4) // 2, (-1, 1)[i % 2])
            else:
                ref = self.ref((i - 12) // 2, 2, i % 2)
            recv(ref, self.sems[0].at[self.p, i], self.sems[1].at[self.p, i])

        def line(self, d):
            self.put(self.ref(d, 0), 4 + 2 * d, self.second(1))
            self.put(self.ref(d, 0), 5 + 2 * d, self.second(-1))

        def own(self):
            self.put(self.ref(0, 0), 0, self.first(1))
            self.put(self.ref(0, 0), 1, self.first(-1))

        def own_line(self):
            self.line(0)

        def up(self):
            self.get(0)
            self.put(self.ref(-1, 0, 0), 2, self.first(1))

        def down(self):
            self.get(1)
            self.put(self.ref(1, 0, 1), 3, self.first(-1))

        def low_line(self):
            self.get(0)
            self.line(3)

        def high_line(self):
            self.get(1)
            self.line(1)

        def far_line(self):
            self.get(2)
            self.get(3)
            self.line(2)

        def up_line(self, d):
            self.get(4 + 2 * d)
            self.put(self.ref(d, -1, 0), 12 + 2 * d, self.second(1))

        def down_line(self, d):
            self.get(5 + 2 * d)
            self.put(self.ref(d, 1, 1), 13 + 2 * d, self.second(-1))

        def need(self, keys):
            for i in keys:
                self.get(i)

    halves = {
        p: (
            Half(p, 0, (a_send, a_recv), at_x, at_y, False),
            Half(p, HALF, (b_send, b_recv), at_y, at_x, True),
        )
        for p in range(2)
    }
    a0, b0 = halves[0]
    a1, b1 = halves[1]

    theirs = pl.ds(pl.multiple_of((1 - core) * KH, KH), KH)
    mine = pl.ds(pl.multiple_of(core * KH, KH), KH)

    first_one = []

    def products_one(half, lo, n):
        half.need(range(20))
        k = slice(lo, lo + n)
        h = H[1, :, :, k].reshape(NB, n)
        s = dot(h, E[k, :])
        c = dot(h, H[0, slot, :, k], ((1,), (1,)))
        w1[...] = s + w1[...] if first_one else s
        ct[...] = c + ct[...] if first_one else c
        first_one.append(lo)

    def send_cross():
        crow[0] = ct[...].T
        for d in range(1, 16):
            send(crow.at[0], crow.at[d], g_send.at[d], g_recv.at[d], {"row": (row + d) % 16})

    first_zero = []

    def products_zero(half, lo, n):
        half.need(range(20))
        k = slice(lo, lo + n)
        w = dot(H[0, :, :, k].reshape(NB, n), E[k, :])
        w0[...] = w + w0[...] if first_zero else w
        first_zero.append(lo)

    def swap(i, w, c):
        send(w.at[:, theirs], c, w_send.at[i], w_recv.at[i], sibling)

    def scatter(i, w, c, xs, zs):
        recv(c, w_send.at[i], w_recv.at[i])
        s = (w[:, mine] + c[...]).T.reshape(4, NZ, 8, NB)
        for g in range(4):
            xs[:, g] = s[g]
        for d in (4, 3, 5, 2, 6, 1, 7):
            send(xs.at[(z + d) % NZ], zs.at[d], z_send.at[i, d], z_recv.at[i, d], at_z(d))

    def collect(i, xs, zs):
        total = xs[z]
        for d in range(1, NZ):
            recv(zs.at[d], z_send.at[i, d], z_recv.at[i, d])
            total = total + zs[d]
        return total.reshape(32, NB)

    def cross_sum():
        total = crow[0]
        for d in range(1, 16):
            recv(crow.at[d], g_send.at[d], g_recv.at[d])
            total = total + crow[d]
        C[slot] = total
        for d in range(1, 16):
            send(C.at[slot], C.at[slot], c_send.at[d], c_recv.at[d], {"col": (col + d) % 16})

    def cross_recv():
        for d in range(1, 16):
            o = (col + 16 - d) % 16
            recv(C.at[(o % NX) * NX + o // NX], c_send.at[d], c_recv.at[d])
        return C[...].reshape(NB, NB)

    def spread(p, value):
        ref = ybuf.at[p, core * NZ + z]
        ybuf[p, core * NZ + z] = value
        for d in (4, 3, 5, 2, 6, 1, 7):
            send(ref, ref, y_send.at[p, d], y_recv.at[p, d], at_z(d))
            if d in FAR:
                send(ref, ref, f_send.at[p, d], f_recv.at[p, d], at_z(d, 1 - core))
        send(ref, ref, f_send.at[p, 0], f_recv.at[p, 0], sibling)

    def pass_on(p):
        for d in (1, 7, 2, 6, 3, 5, 4):
            ref = ybuf.at[p, core * NZ + (z + NZ - d) % NZ]
            recv(ref, y_send.at[p, d], y_recv.at[p, d])
            if d not in FAR:
                send(ref, ref, f_send.at[p, d], f_recv.at[p, d], sibling)

    def place(p, c):
        v = [ybuf[p, c * NZ + i].astype(F32) for i in range(NZ)]
        v = jnp.concatenate([v[i][g * 8 : g * 8 + 8, :] for g in range(4) for i in range(NZ)], axis=0)
        Y[p * NB : (p + 1) * NB, pl.ds(pl.multiple_of(c * KH, KH), KH)] = v.T.astype(BF16)

    def finish(p):
        place(p, core)
        for d in range(NZ):
            recv(ybuf.at[p, (1 - core) * NZ + (z + NZ - d) % NZ], f_send.at[p, d], f_recv.at[p, d])
        place(p, 1 - core)

    def turn(p):
        for r in range(0, RD, 512):
            HT[r : r + 512, p * NB : (p + 1) * NB] = H[p, :, :, r : r + 512].reshape(NB, 512).T

    def upper_factors():
        load_tf.wait()
        tri = lax.broadcasted_iota(jnp.int32, (NB, NB), 0) <= lax.broadcasted_iota(jnp.int32, (NB, NB), 1)
        for p in range(2):
            T[p] = by_place(by_place(jnp.where(tri, tfbuf[p], 0.0)).T)

    a1.own()
    b1.own()
    a0.own()
    b0.own_line()
    a1.own_line()
    b0.own()
    b1.own_line()
    upper_factors()
    b1.low_line()
    b1.up()
    b1.down()
    a0.own_line()
    a1.up()
    b1.high_line()
    a1.down()
    a1.low_line()
    a1.up_line(0)
    a0.up()
    a0.down()
    a1.high_line()
    a0.high_line()
    b1.far_line()
    a0.low_line()
    b0.high_line()
    b1.up_line(0)
    b1.down_line(3)
    b1.up_line(3)
    b0.low_line()
    b0.down()
    b0.up()
    b1.down_line(1)
    a1.far_line()
    a0.far_line()
    a1.up_line(3)
    a1.down_line(3)
    a1.down_line(1)
    a1.down_line(0)
    a0.up_line(0)
    b1.down_line(2)
    b1.up_line(1)
    b1.up_line(2)
    b1.down_line(0)
    a1.up_line(1)
    b0.far_line()
    b0.up_line(0)
    a1.up_line(2)
    b0.down_line(0)
    a1.down_line(2)
    a0.down_line(1)
    a0.up_line(1)
    b0.up_line(3)
    b0.down_line(1)
    a0.up_line(3)
    a0.down_line(3)
    b0.down_line(3)
    a0.up_line(2)
    b0.up_line(1)
    a0.down_line(0)
    a0.down_line(2)
    load_eig.wait()
    products_one(b1, HALF, HALF)
    b0.down_line(2)
    b0.up_line(2)
    products_one(a1, 0, HALF)
    send_cross()
    swap(1, w1, c1)
    products_zero(a0, 0, HALF)
    scatter(1, w1, c1, x1, z1)
    products_zero(b0, HALF, HALF)
    swap(0, w0, c0)
    scatter(0, w0, c0, x0, z0)
    cross_sum()
    y1 = dot(collect(1, x1, z1), T[1], precision=HIGH).astype(BF16)
    spread(1, y1)
    turn(1)
    turn(0)
    cross = cross_recv()
    shift = dot(y1.astype(F32), cross, ((1,), (1,)), precision=HIGH)
    total = collect(0, x0, z0)
    spread(0, dot(total - shift, T[0], precision=HIGH).astype(BF16))
    pass_on(1)
    finish(1)
    settle()
    pass_on(0)
    finish(0)
    settle()


ROWS = 512


def apply_shift(HT, Y, E, out, done, sems):
    copies = []
    for i in range(RD // ROWS):
        rows = slice(i * ROWS, (i + 1) * ROWS)
        done[rows, :] = (E[rows, :].astype(F32) - dot(HT[rows, :], Y[...])).astype(BF16)
        copies.append(pltpu.make_async_copy(done.at[rows, :], out.at[rows, :], sems.at[i]))
        copies[-1].start()
    for cp in copies:
        cp.wait()


def local(eigvecs, panels, tfactors, offsets):
    hbm = pl.BlockSpec(memory_space=pltpu.HBM)
    dma = pltpu.SemaphoreType.DMA
    HT, Y, E = pl.pallas_call(
        gather_and_reduce,
        out_shape=[
            pltpu.VMEM((RD, 2 * NB), BF16),
            pltpu.VMEM((2 * NB, KD), BF16),
            pltpu.VMEM((RD, KD), BF16),
        ],
        in_specs=[hbm] * 4,
        out_specs=[pl.BlockSpec(memory_space=pltpu.VMEM)] * 3,
        scratch_shapes=[
            pltpu.VMEM((2, SLOTS, OWN, RD), BF16),
            pltpu.SMEM((2,), jnp.int32),
            pltpu.VMEM((2, OWN, RD), BF16),
            pltpu.VMEM((2, NB, NB), F32),
            pltpu.VMEM((2, NB, NB), F32),
            pltpu.VMEM((NB, OWN), F32),
            pltpu.VMEM((NB, KD), F32),
            pltpu.VMEM((NB, KH), F32),
            pltpu.VMEM((NZ, 4, 8, NB), F32),
            pltpu.VMEM((NZ, 4, 8, NB), F32),
            pltpu.VMEM((NB, KD), F32),
            pltpu.VMEM((NB, KH), F32),
            pltpu.VMEM((NZ, 4, 8, NB), F32),
            pltpu.VMEM((NZ, 4, 8, NB), F32),
            pltpu.VMEM((16, OWN, NB), F32),
            pltpu.VMEM((SLOTS, OWN, NB), F32),
            pltpu.VMEM((2, 16, 32, NB), BF16),
            dma((4,)),
            dma((2, 20)), dma((2, 20)), dma((2, 20)), dma((2, 20)),
            dma((2,)), dma((2,)),
            dma((2, NZ)), dma((2, NZ)),
            dma((16,)), dma((16,)), dma((16,)), dma((16,)),
            dma((2, NZ)), dma((2, NZ)),
            dma((2, NZ)), dma((2, NZ)),
        ],
        compiler_params=pltpu.CompilerParams(
            collective_id=0, has_side_effects=True, vmem_limit_bytes=40 * 1024 * 1024
        ),
        name="gather_and_reduce",
    )(*(pltpu.with_memory_space_constraint(v, pltpu.HBM) for v in (offsets, panels, eigvecs, tfactors)))
    whole = pl.BlockSpec(memory_space=pltpu.VMEM)
    return pl.pallas_call(
        apply_shift,
        out_shape=jax.ShapeDtypeStruct((RD, KD), BF16),
        in_specs=[whole, whole, whole],
        out_specs=hbm,
        scratch_shapes=[pltpu.VMEM((RD, KD), BF16), dma((RD // ROWS,))],
        compiler_params=pltpu.CompilerParams(vmem_limit_bytes=40 * 1024 * 1024),
        name="apply_shift",
    )(HT, Y, E)


def solution(mesh):
    return jax.shard_map(
        local,
        mesh=mesh,
        in_specs=(P("row", "col"), P(None, "col", "row"), P(), P()),
        out_specs=P("row", "col"),
        check_vma=False,
    )
```

```python
import jax
import jax.numpy as jnp
from jax import lax
from jax.experimental import pallas as pl
from jax.experimental.pallas import tpu as pltpu
from jax.sharding import PartitionSpec as P

MESH = pl.DeviceIdType.MESH
F32 = jnp.float32
BF16 = jnp.bfloat16
HIGH = lax.Precision.HIGHEST

NB = 128
RD = 6144
KD = 512
KH = KD // 2
NX = 4
NZ = 8
OWN = 8
SLOTS = NX * NX
FAR = (4,)
HALF = RD // 2
QUART = RD // 4


def dot(a, b, dims=((1,), (0,)), precision=None):
    return lax.dot_general(a, b, (dims, ((), ())), precision=precision, preferred_element_type=F32)


def by_place(a):
    return jnp.concatenate([a[(sy * NX + sx) * OWN :][:OWN, :] for sx in range(NX) for sy in range(NX)], axis=0)


def gather_and_reduce(
    offsets, panels, eig, tf, HT, Y, E,
    H, obuf, pbuf, tfbuf, T, ct, w1, c1, x1, z1, w0, c0, x0, z0, crow, C, ybuf,
    local_sem, a_send, a_recv, b_send, b_recv,
    w_send, w_recv, z_send, z_recv, g_send, g_recv, c_send, c_recv, y_send, y_recv, f_send, f_recv,
):
    col = lax.axis_index("col")
    row = lax.axis_index("row")
    x, y = col % NX, col // NX
    z, core = row // 2, row % 2

    def at_x(d):
        return {"col": y * NX + (x + d) % NX}

    def at_y(d):
        return {"col": ((y + d) % NX) * NX + x}

    def at_z(d, c=core):
        return {"row": ((z + d) % NZ) * 2 + c}

    sibling = {"row": z * 2 + (1 - core)}

    load_panels = pltpu.make_async_copy(panels, pbuf, local_sem.at[0])
    load_offsets = pltpu.make_async_copy(offsets, obuf, local_sem.at[3])
    load_tf = pltpu.make_async_copy(tf, tfbuf, local_sem.at[1])
    load_eig = pltpu.make_async_copy(eig, E, local_sem.at[2])
    load_panels.start()
    load_offsets.start()
    load_tf.start()
    load_eig.start()

    barrier = pltpu.get_barrier_semaphore()
    for d in range(1, 16):
        pl.semaphore_signal(barrier, inc=1, device_id={"col": (col + d) % 16}, device_id_type=MESH)
        pl.semaphore_signal(barrier, inc=1, device_id={"row": (row + d) % 16}, device_id_type=MESH)

    slot = x * NX + y
    load_panels.wait()
    load_offsets.wait()
    step = 512
    for p in range(2):
        pivot = obuf[p] + col * OWN + lax.broadcasted_iota(jnp.int32, (OWN, step), 0)
        for s in range(0, RD, step):
            position = row * RD + s + lax.broadcasted_iota(jnp.int32, (OWN, step), 1)
            v = pbuf[p, :, s : s + step].astype(F32)
            v = jnp.where(position > pivot, v, jnp.where(position == pivot, 1.0, 0.0))
            H[p, slot, :, s : s + step] = v.astype(BF16)

    pl.semaphore_wait(barrier, 30)

    def part(p, dx, dy, lo, n):
        return H.at[p, ((x + dx) % NX) * NX + (y + dy) % NX, :, lo : lo + n]

    sent = []

    def send(src, dst, send_sem, recv_sem, dev):
        cp = pltpu.make_async_remote_copy(src, dst, send_sem, recv_sem, device_id=dev, device_id_type=MESH)
        cp.start()
        sent.append(cp)

    def settle():
        for cp in sent:
            cp.wait_send()
        sent.clear()

    def recv(ref, send_sem, recv_sem):
        pltpu.make_async_remote_copy(
            ref, ref, send_sem, recv_sem, device_id=sibling, device_id_type=MESH
        ).wait_recv()

    class Half:
        def __init__(self, p, lo, sems, first, second, turn):
            self.p, self.lo, self.sems = p, lo, sems
            self.first, self.second, self.turn = first, second, turn
            self.got = set()

        def ref(self, d1, d2, piece=None):
            lo, n = (self.lo, HALF) if piece is None else (self.lo + piece * QUART, QUART)
            return part(self.p, d2, d1, lo, n) if self.turn else part(self.p, d1, d2, lo, n)

        def put(self, ref, i, dev):
            send(ref, ref, self.sems[0].at[self.p, i], self.sems[1].at[self.p, i], dev)

        def get(self, i):
            if i in self.got:
                return
            self.got.add(i)
            if i < 2:
                ref = self.ref((-1, 1)[i], 0)
            elif i < 4:
                ref = self.ref(2, 0, i - 2)
            elif i < 12:
                ref = self.ref((i - 4) // 2, (-1, 1)[i % 2])
            else:
                ref = self.ref((i - 12) // 2, 2, i % 2)
            recv(ref, self.sems[0].at[self.p, i], self.sems[1].at[self.p, i])

        def line(self, d):
            self.put(self.ref(d, 0), 4 + 2 * d, self.second(1))
            self.put(self.ref(d, 0), 5 + 2 * d, self.second(-1))

        def own(self):
            self.put(self.ref(0, 0), 0, self.first(1))
            self.put(self.ref(0, 0), 1, self.first(-1))

        def own_line(self):
            self.line(0)

        def up(self):
            self.get(0)
            self.put(self.ref(-1, 0, 0), 2, self.first(1))

        def down(self):
            self.get(1)
            self.put(self.ref(1, 0, 1), 3, self.first(-1))

        def low_line(self):
            self.get(0)
            self.line(3)

        def high_line(self):
            self.get(1)
            self.line(1)

        def far_line(self):
            self.get(2)
            self.get(3)
            self.line(2)

        def up_line(self, d):
            self.get(4 + 2 * d)
            self.put(self.ref(d, -1, 0), 12 + 2 * d, self.second(1))

        def down_line(self, d):
            self.get(5 + 2 * d)
            self.put(self.ref(d, 1, 1), 13 + 2 * d, self.second(-1))

        def need(self, keys):
            for i in keys:
                self.get(i)

    halves = {
        p: (
            Half(p, 0, (a_send, a_recv), at_x, at_y, False),
            Half(p, HALF, (b_send, b_recv), at_y, at_x, True),
        )
        for p in range(2)
    }
    a0, b0 = halves[0]
    a1, b1 = halves[1]

    theirs = pl.ds(pl.multiple_of((1 - core) * KH, KH), KH)
    mine = pl.ds(pl.multiple_of(core * KH, KH), KH)

    first_one = []

    def products_one(half, lo, n):
        half.need(range(20))
        k = slice(lo, lo + n)
        h = H[1, :, :, k].reshape(NB, n)
        s = dot(h, E[k, :])
        c = dot(h, H[0, slot, :, k], ((1,), (1,)))
        w1[...] = s + w1[...] if first_one else s
        ct[...] = c + ct[...] if first_one else c
        first_one.append(lo)

    def send_cross():
        crow[0] = ct[...].T
        for d in range(1, 16):
            send(crow.at[0], crow.at[d], g_send.at[d], g_recv.at[d], {"row": (row + d) % 16})

    first_zero = []

    def products_zero(half, lo, n):
        half.need(range(20))
        k = slice(lo, lo + n)
        w = dot(H[0, :, :, k].reshape(NB, n), E[k, :])
        w0[...] = w + w0[...] if first_zero else w
        first_zero.append(lo)

    def swap(i, w, c):
        send(w.at[:, theirs], c, w_send.at[i], w_recv.at[i], sibling)

    def scatter(i, w, c, xs, zs):
        recv(c, w_send.at[i], w_recv.at[i])
        s = (w[:, mine] + c[...]).T.reshape(4, NZ, 8, NB)
        for g in range(4):
            xs[:, g] = s[g]
        for d in (4, 3, 5, 2, 6, 1, 7):
            send(xs.at[(z + d) % NZ], zs.at[d], z_send.at[i, d], z_recv.at[i, d], at_z(d))

    def collect(i, xs, zs):
        total = xs[z]
        for d in range(1, NZ):
            recv(zs.at[d], z_send.at[i, d], z_recv.at[i, d])
            total = total + zs[d]
        return total.reshape(32, NB)

    def cross_sum():
        total = crow[0]
        for d in range(1, 16):
            recv(crow.at[d], g_send.at[d], g_recv.at[d])
            total = total + crow[d]
        C[slot] = total
        for d in range(1, 16):
            send(C.at[slot], C.at[slot], c_send.at[d], c_recv.at[d], {"col": (col + d) % 16})

    def cross_recv():
        for d in range(1, 16):
            o = (col + 16 - d) % 16
            recv(C.at[(o % NX) * NX + o // NX], c_send.at[d], c_recv.at[d])
        return C[...].reshape(NB, NB)

    def spread(p, value):
        ref = ybuf.at[p, core * NZ + z]
        ybuf[p, core * NZ + z] = value
        for d in (4, 3, 5, 2, 6, 1, 7):
            send(ref, ref, y_send.at[p, d], y_recv.at[p, d], at_z(d))
            if d in FAR:
                send(ref, ref, f_send.at[p, d], f_recv.at[p, d], at_z(d, 1 - core))
        send(ref, ref, f_send.at[p, 0], f_recv.at[p, 0], sibling)

    def pass_on(p):
        for d in (1, 7, 2, 6, 3, 5, 4):
            ref = ybuf.at[p, core * NZ + (z + NZ - d) % NZ]
            recv(ref, y_send.at[p, d], y_recv.at[p, d])
            if d not in FAR:
                send(ref, ref, f_send.at[p, d], f_recv.at[p, d], sibling)

    def place(p, c):
        v = [ybuf[p, c * NZ + i].astype(F32) for i in range(NZ)]
        v = jnp.concatenate([v[i][g * 8 : g * 8 + 8, :] for g in range(4) for i in range(NZ)], axis=0)
        Y[p * NB : (p + 1) * NB, pl.ds(pl.multiple_of(c * KH, KH), KH)] = v.T.astype(BF16)

    def finish(p):
        place(p, core)
        for d in range(NZ):
            recv(ybuf.at[p, (1 - core) * NZ + (z + NZ - d) % NZ], f_send.at[p, d], f_recv.at[p, d])
        place(p, 1 - core)

    def turn(p):
        for r in range(0, RD, 512):
            HT[r : r + 512, p * NB : (p + 1) * NB] = H[p, :, :, r : r + 512].reshape(NB, 512).T

    def upper_factors():
        load_tf.wait()
        tri = lax.broadcasted_iota(jnp.int32, (NB, NB), 0) <= lax.broadcasted_iota(jnp.int32, (NB, NB), 1)
        for p in range(2):
            T[p] = by_place(by_place(jnp.where(tri, tfbuf[p], 0.0)).T)

    a1.own()
    b1.own()
    a0.own()
    b0.own_line()
    a1.own_line()
    b0.own()
    b1.own_line()
    upper_factors()
    b1.low_line()
    b1.up()
    b1.down()
    a0.own_line()
    a1.up()
    b1.high_line()
    a1.down()
    a1.low_line()
    a1.up_line(0)
    a0.up()
    a0.down()
    a1.high_line()
    a0.high_line()
    b1.far_line()
    a0.low_line()
    b0.high_line()
    b1.up_line(0)
    b1.down_line(3)
    b1.up_line(3)
    b0.low_line()
    b0.down()
    b0.up()
    b1.down_line(1)
    a1.far_line()
    a0.far_line()
    a1.up_line(3)
    a1.down_line(3)
    a1.down_line(1)
    a1.down_line(0)
    a0.up_line(0)
    b1.down_line(2)
    b1.up_line(1)
    b1.up_line(2)
    b1.down_line(0)
    a1.up_line(1)
    b0.far_line()
    b0.up_line(0)
    a1.up_line(2)
    b0.down_line(0)
    a1.down_line(2)
    a0.down_line(1)
    a0.up_line(1)
    b0.up_line(3)
    b0.down_line(1)
    a0.up_line(3)
    a0.down_line(3)
    b0.down_line(3)
    a0.up_line(2)
    b0.up_line(1)
    a0.down_line(0)
    a0.down_line(2)
    load_eig.wait()
    products_one(b1, HALF, HALF)
    b0.down_line(2)
    b0.up_line(2)
    products_one(a1, 0, HALF)
    swap(1, w1, c1)
    send_cross()
    products_zero(a0, 0, HALF)
    scatter(1, w1, c1, x1, z1)
    products_zero(b0, HALF, HALF)
    swap(0, w0, c0)
    scatter(0, w0, c0, x0, z0)
    cross_sum()
    y1 = dot(collect(1, x1, z1), T[1], precision=HIGH).astype(BF16)
    spread(1, y1)
    turn(1)
    turn(0)
    cross = cross_recv()
    shift = dot(y1.astype(F32), cross, ((1,), (1,)), precision=HIGH)
    total = collect(0, x0, z0)
    spread(0, dot(total - shift, T[0], precision=HIGH).astype(BF16))
    pass_on(1)
    finish(1)
    settle()
    pass_on(0)
    finish(0)
    settle()


ROWS = 512


def apply_shift(HT, Y, E, out, done, sems):
    copies = []
    for i in range(RD // ROWS):
        rows = slice(i * ROWS, (i + 1) * ROWS)
        done[rows, :] = (E[rows, :].astype(F32) - dot(HT[rows, :], Y[...])).astype(BF16)
        copies.append(pltpu.make_async_copy(done.at[rows, :], out.at[rows, :], sems.at[i]))
        copies[-1].start()
    for cp in copies:
        cp.wait()


def local(eigvecs, panels, tfactors, offsets):
    hbm = pl.BlockSpec(memory_space=pltpu.HBM)
    dma = pltpu.SemaphoreType.DMA
    HT, Y, E = pl.pallas_call(
        gather_and_reduce,
        out_shape=[
            pltpu.VMEM((RD, 2 * NB), BF16),
            pltpu.VMEM((2 * NB, KD), BF16),
            pltpu.VMEM((RD, KD), BF16),
        ],
        in_specs=[hbm] * 4,
        out_specs=[pl.BlockSpec(memory_space=pltpu.VMEM)] * 3,
        scratch_shapes=[
            pltpu.VMEM((2, SLOTS, OWN, RD), BF16),
            pltpu.SMEM((2,), jnp.int32),
            pltpu.VMEM((2, OWN, RD), BF16),
            pltpu.VMEM((2, NB, NB), F32),
            pltpu.VMEM((2, NB, NB), F32),
            pltpu.VMEM((NB, OWN), F32),
            pltpu.VMEM((NB, KD), F32),
            pltpu.VMEM((NB, KH), F32),
            pltpu.VMEM((NZ, 4, 8, NB), F32),
            pltpu.VMEM((NZ, 4, 8, NB), F32),
            pltpu.VMEM((NB, KD), F32),
            pltpu.VMEM((NB, KH), F32),
            pltpu.VMEM((NZ, 4, 8, NB), F32),
            pltpu.VMEM((NZ, 4, 8, NB), F32),
            pltpu.VMEM((16, OWN, NB), F32),
            pltpu.VMEM((SLOTS, OWN, NB), F32),
            pltpu.VMEM((2, 16, 32, NB), BF16),
            dma((4,)),
            dma((2, 20)), dma((2, 20)), dma((2, 20)), dma((2, 20)),
            dma((2,)), dma((2,)),
            dma((2, NZ)), dma((2, NZ)),
            dma((16,)), dma((16,)), dma((16,)), dma((16,)),
            dma((2, NZ)), dma((2, NZ)),
            dma((2, NZ)), dma((2, NZ)),
        ],
        compiler_params=pltpu.CompilerParams(
            collective_id=0, has_side_effects=True, vmem_limit_bytes=40 * 1024 * 1024
        ),
        name="gather_and_reduce",
    )(*(pltpu.with_memory_space_constraint(v, pltpu.HBM) for v in (offsets, panels, eigvecs, tfactors)))
    whole = pl.BlockSpec(memory_space=pltpu.VMEM)
    return pl.pallas_call(
        apply_shift,
        out_shape=jax.ShapeDtypeStruct((RD, KD), BF16),
        in_specs=[whole, whole, whole],
        out_specs=hbm,
        scratch_shapes=[pltpu.VMEM((RD, KD), BF16), dma((RD // ROWS,))],
        compiler_params=pltpu.CompilerParams(vmem_limit_bytes=40 * 1024 * 1024),
        name="apply_shift",
    )(HT, Y, E)


def solution(mesh):
    return jax.shard_map(
        local,
        mesh=mesh,
        in_specs=(P("row", "col"), P(None, "col", "row"), P(), P()),
        out_specs=P("row", "col"),
        check_vma=False,
    )
```
